32 devices in a mesh: gx: 4 (over y, x), gy: 8 (over z, core).
Axes of the slice: x: 2, y: 2, z: 4, core: 2. Of those that a mesh axis runs over, the one named last changes fastest.
Arguments:
- electric: float32 [3, 64, 64, 256], P(None, 'gx', 'gy'), may hold values from -1.5 to 1.5
- magnetic: float32 [3, 64, 64, 256], P(None, 'gx', 'gy'), may hold values from -6 to 6
- material: int32 [64, 64, 256], P('gx', 'gy'), may hold values from 0 to 7
- permittivity: float32 [8], replicated, may hold values from 1 to 4
- conductivity: float32 [8], replicated, may hold values from 0.01 to 1
Outputs:
- advanced_electric: float32 [3, 64, 64, 256], P(None, 'gx', 'gy')
- advanced_magnetic: float32 [3, 64, 64, 256], P(None, 'gx', 'gy')
The draws below stay inside these ranges and needn't reach their ends.
All inputs are finite; a program needn't handle non-finite values.
Results may differ from the reference program's by a relative error of at most 0.0003.
Values sent between devices are 32-bit elements; how exact they have to be, the bound alone decides.
A program may use at most 64 MiB of HBM per device.

```python
import math
import jax
import jax.numpy as jnp
from jax import lax

CZ = 256
NMAT = 8
NX = 64
NY = 64


def plant(values, own_key, low, top_value):
    longest = values.shape.index(max(values.shape))
    spots = []
    for shift in (0, 1):
        where = [jax.random.randint(jax.random.fold_in(own_key, axis), (), 0, length) for axis, length in enumerate(values.shape)]
        where[longest] = (where[longest] + shift) % values.shape[longest]
        spots.append(tuple(where))
    return values.at[spots[0]].set(low).at[spots[1]].set(top_value)


def block_scale(stream_key, shape, shards, low, top_value):
    gain, own = 1.0, jax.random.fold_in(stream_key, 6)
    for axis_at, shards_of in shards:
        heights = jnp.exp(jax.random.uniform(jax.random.fold_in(own, axis_at), (shards_of,), jnp.float32, low / len(shards), top_value / len(shards)))
        gain = gain * jnp.repeat(heights, shape[axis_at] // shards_of).reshape([-1 if axis == axis_at else 1 for axis in range(len(shape))])
    return gain


def normal_values(own_key, dims, width, most, shards=(), held_as=jnp.bfloat16):
    factor_of = block_scale(own_key, dims, shards, -0.22, 0.18) if shards else 1.0
    array = jax.random.normal(own_key, dims, jnp.float32) * width * factor_of
    return jnp.minimum(jnp.maximum(array, -most), most).astype(held_as)


def setup_inputs(seed: int = 0) -> dict:
    key_list = jax.random.split(jax.random.key(seed), 6)
    return {
        "electric": normal_values(key_list[0], (3, NX, NY, CZ), 0.25, 1.5, ((1, 4), (2, 8)), jnp.float32),
        "magnetic": normal_values(key_list[1], (3, NX, NY, CZ), 1.0, 6.0, ((1, 4), (2, 8)), jnp.float32),
        "material": plant(jax.random.randint(key_list[2], (NX, NY, CZ), 0, NMAT), jax.random.fold_in(key_list[2], 1), 0, NMAT - 1).astype(jnp.int32),
        "permittivity": jnp.clip(jnp.exp(jax.random.uniform(key_list[3], (NMAT,), jnp.float32, math.log(1.0), math.log(4.0))), 1.0, 4.0),
        "conductivity": jnp.clip(jnp.exp(jax.random.uniform(key_list[4], (NMAT,), jnp.float32, math.log(0.01), math.log(1.0))), 0.01, 1.0),
    }


half_step = 12.0


def forward_diff(field, line_axis):
    length = field.shape[line_axis]
    zero_plane = jnp.zeros_like(lax.slice_in_dim(field, 0, 1, axis=line_axis))
    shifted = jnp.concatenate([lax.slice_in_dim(field, 1, length, axis=line_axis), zero_plane], axis=line_axis)
    return shifted - field


def backward_diff(field, line_axis):
    length = field.shape[line_axis]
    zero_plane = jnp.zeros_like(lax.slice_in_dim(field, 0, 1, axis=line_axis))
    shifted = jnp.concatenate([zero_plane, lax.slice_in_dim(field, 0, length - 1, axis=line_axis)], axis=line_axis)
    return field - shifted


def build_system(source, stiffness, position, line_length):
    below = jnp.where(position == 0, 0.0, -stiffness)
    above = jnp.where(position == line_length - 1, 0.0, -stiffness)
    diagonal = jnp.where(position == 0, 1.0 + stiffness, 1.0 + 2.0 * stiffness)
    return jnp.stack([below, diagonal, above, source])


def reduce_level(system, preceding, following):
    divisor_below = jnp.where(preceding[1] == 0.0, 1.0, preceding[1])
    divisor_above = jnp.where(following[1] == 0.0, 1.0, following[1])
    factor_below = -system[0] / divisor_below
    factor_above = -system[2] / divisor_above
    return jnp.stack([
        factor_below * preceding[0],
        system[1] + factor_below * preceding[2] + factor_above * following[0],
        factor_above * following[2],
        system[3] + factor_below * preceding[3] + factor_above * following[3],
    ])


def shift_local(system, stride, stack_axis, from_before):
    length = system.shape[stack_axis]
    zero_block = jnp.zeros_like(lax.slice_in_dim(system, 0, stride, axis=stack_axis))
    if from_before:
        return jnp.concatenate([zero_block, lax.slice_in_dim(system, 0, length - stride, axis=stack_axis)], axis=stack_axis)
    return jnp.concatenate([lax.slice_in_dim(system, stride, length, axis=stack_axis), zero_block], axis=stack_axis)


def solve_local(source, stiffness, line_axis):
    length = source.shape[line_axis]
    position = lax.broadcasted_iota(jnp.int32, source.shape, line_axis)
    system = build_system(source, stiffness, position, length)
    stride = 1
    while stride < length:
        system = reduce_level(system, shift_local(system, stride, line_axis + 1, True),
                              shift_local(system, stride, line_axis + 1, False))
        stride = stride * 2
    return system[3] / system[1]


def coefficients(permittivity, conductivity):
    denom_table = permittivity / half_step + 0.5 * conductivity
    damp_table = (permittivity / half_step - 0.5 * conductivity) / denom_table
    couple_table = 1.0 / denom_table
    return damp_table, couple_table


def reference(electric, magnetic, material, permittivity, conductivity):
    damp_table, couple_table = coefficients(permittivity, conductivity)
    damping = damp_table[material]
    coupling = couple_table[material]
    stiffness = half_step * coupling
    interim_z = magnetic[2] - half_step * forward_diff(electric[1], 0)
    interim_x = magnetic[0] - half_step * forward_diff(electric[2], 1)
    interim_y = magnetic[1] - half_step * forward_diff(electric[0], 2)
    center_x = solve_local(damping * electric[0] + coupling * (backward_diff(interim_z, 1) - backward_diff(magnetic[1], 2)), stiffness, 1)
    center_y = solve_local(damping * electric[1] + coupling * (backward_diff(interim_x, 2) - backward_diff(magnetic[2], 0)), stiffness, 2)
    center_z = solve_local(damping * electric[2] + coupling * (backward_diff(interim_y, 0) - backward_diff(magnetic[0], 1)), stiffness, 0)
    curl_for_z = half_step * forward_diff(center_x, 1)
    curl_for_x = half_step * forward_diff(center_y, 2)
    curl_for_y = half_step * forward_diff(center_z, 0)
    middle_z = interim_z + curl_for_z
    middle_x = interim_x + curl_for_x
    middle_y = interim_y + curl_for_y
    second_z = middle_z + curl_for_z
    second_x = middle_x + curl_for_x
    second_y = middle_y + curl_for_y
    final_x = solve_local(damping * center_x + coupling * (backward_diff(middle_z, 1) - backward_diff(second_y, 2)), stiffness, 2)
    final_y = solve_local(damping * center_y + coupling * (backward_diff(middle_x, 2) - backward_diff(second_z, 0)), stiffness, 0)
    final_z = solve_local(damping * center_z + coupling * (backward_diff(middle_y, 0) - backward_diff(second_x, 1)), stiffness, 1)
    magnet_z = second_z - half_step * forward_diff(final_y, 0)
    magnet_x = second_x - half_step * forward_diff(final_z, 1)
    magnet_y = second_y - half_step * forward_diff(final_x, 2)
    return jnp.stack([final_x, final_y, final_z]), jnp.stack([magnet_x, magnet_y, magnet_z])
```

```python
import functools

import jax
import jax.numpy as jnp
from jax import lax
from jax.experimental import pallas as pl
from jax.experimental.pallas import tpu as pltpu
from jax.sharding import PartitionSpec as P

half_step = 12.0
MESH = pl.DeviceIdType.MESH


def strides(length):
    found, stride = [], 1
    while stride < length:
        found.append(stride)
        stride *= 2
    return found


def shift(v, by, axis):
    if axis == 0:
        zero = jnp.zeros((abs(by),) + v.shape[1:], v.dtype)
        if by > 0:
            return jnp.concatenate([zero, v[:-by]], axis=0)
        return jnp.concatenate([v[-by:], zero], axis=0)
    return pltpu.roll(v, by % v.shape[axis], axis)


def position(shape, axis):
    return lax.broadcasted_iota(jnp.int32, shape, axis)


def factor(diagonal, axis, factors):
    length = diagonal.shape[axis]
    above = jnp.where(position(diagonal.shape, axis) == length - 1, 0.0, -1.0)
    for level, stride in enumerate(strides(length)):
        inverse = 1.0 / diagonal
        below = shift(above, stride, axis)
        from_below = -below * shift(inverse, stride, axis)
        from_above = -above * shift(inverse, -stride, axis)
        factors[2 * level] = from_below
        factors[2 * level + 1] = from_above
        diagonal = diagonal + from_below * below + from_above * above
        if 2 * stride < length:
            above = from_above * shift(above, -stride, axis)
    factors[factors.shape[0] - 1] = 1.0 / diagonal


def apply(source, axis, factors):
    for level, stride in enumerate(strides(source.shape[axis])):
        source = (
            source
            + factors[2 * level] * shift(source, stride, axis)
            + factors[2 * level + 1] * shift(source, -stride, axis)
        )
    return source * factors[factors.shape[0] - 1]


def sweep_matrix(first, cross, last):
    gain, pivots, mults, gains = jnp.zeros_like(first[0]), [], [], []
    for k in range(len(first)):
        pivot = 1.0 / (1.0 - first[k] * gain)
        mult = cross[k] * pivot
        pivots.append(pivot)
        mults.append(mult)
        gains.append(gain)
        gain = last[k] + mult * gain * cross[k]
    gains.append(gain)
    return pivots, mults, gains


def sweep(first, cross, matrix, w_first, w_last):
    pivots, mults, gains = matrix
    count = len(first)
    sums = [jnp.zeros_like(w_first[0])]
    for k in range(count):
        sums.append(w_last[k] + mults[k] * (sums[k] + gains[k] * w_first[k]))
    p, q = [None] * count, [None] * (count + 1)
    q[count] = jnp.zeros_like(w_first[0])
    for k in reversed(range(count)):
        p[k] = sums[k + 1] + gains[k + 1] * q[k + 1]
        q[k] = pivots[k] * (w_first[k] + first[k] * sums[k] + cross[k] * q[k + 1])
    return p, q


def kernel(
    nx, ny,
    e_ref, h_ref, mat_ref, eps_ref, sig_ref, eo_ref, ho_ref,
    fx, fy, fz, vlx, vrx, vly, vry,
    halo_xs, halo_ys, halo_xr, halo_yr,
    xm_s, xm_r, xa_s, xa_r, ym_s, ym_r, ya_s, ya_r, yb_s, yb_r,
    p_ref, q_ref, pq_ref, w_ref,
    halo_send, halo_recv, x_send, x_recv, y_send, y_recv,
):
    cx, cy, cz = mat_ref.shape
    rows = cx // ny
    ix, iy = lax.axis_index("gx"), lax.axis_index("gy")
    x_others = [(d, lax.rem(ix + d, nx)) for d in range(1, nx)]
    y_others = [(d, lax.rem(iy + d, ny)) for d in range(1, ny)]

    halo_xr[...] = jnp.zeros_like(halo_xr)
    halo_yr[...] = jnp.zeros_like(halo_yr)
    barrier = pltpu.get_barrier_semaphore()
    for _, other in x_others:
        pl.semaphore_signal(barrier, inc=1, device_id=(other, iy), device_id_type=MESH)
    for _, other in y_others:
        pl.semaphore_signal(barrier, inc=1, device_id=(ix, other), device_id_type=MESH)

    halo_xs[0] = e_ref[1, 0]
    halo_xs[1] = h_ref[2, cx - 1]
    halo_ys[0] = e_ref[2, :, 0, :]
    halo_ys[1] = h_ref[0, :, cy - 1, :]

    material = mat_ref[...]
    excess = jnp.zeros(material.shape, jnp.float32)
    carry = jnp.zeros(material.shape, jnp.float32)
    for row in range(eps_ref.shape[0]):
        permit = eps_ref[row] * (1.0 / half_step)
        lossy = sig_ref[row] * 0.5
        chosen = material == row
        excess = jnp.where(chosen, (permit + lossy) * (1.0 / half_step), excess)
        carry = jnp.where(chosen, (permit - lossy) * (1.0 / half_step), carry)

    pl.semaphore_wait(barrier, nx + ny - 2)

    def halo(src, dst, k, to):
        return pltpu.make_async_remote_copy(
            src_ref=src, dst_ref=dst, send_sem=halo_send.at[k], recv_sem=halo_recv.at[k],
            device_id=to, device_id_type=MESH,
        )

    halos = [
        (halo(halo_xs.at[0], halo_xr.at[0], 0, (lax.rem(ix + nx - 1, nx), iy)), ix > 0, ix < nx - 1),
        (halo(halo_xs.at[1], halo_xr.at[1], 1, (lax.rem(ix + 1, nx), iy)), ix < nx - 1, ix > 0),
        (halo(halo_ys.at[0], halo_yr.at[0], 2, (ix, lax.rem(iy + ny - 1, ny))), iy > 0, iy < ny - 1),
        (halo(halo_ys.at[1], halo_yr.at[1], 3, (ix, lax.rem(iy + 1, ny))), iy < ny - 1, iy > 0),
    ]
    for copy, sends, _ in halos:
        pl.when(sends)(copy.start)

    def x_copy(src, buffer, phase, d, owner, to):
        return pltpu.make_async_remote_copy(
            src_ref=src, dst_ref=buffer.at[owner], send_sem=x_send.at[phase, d],
            recv_sem=x_recv.at[phase, owner], device_id=(to, iy), device_id_type=MESH,
        )

    def x_start(src, buffer, phase):
        for d, other in x_others:
            x_copy(src, buffer, phase, d, ix, other).start()
        buffer[ix] = src[...]

    def x_wait(src, buffer, phase):
        for d, other in x_others:
            x_copy(src, buffer, phase, d, other, other).wait_recv()

    def y_copy(src, buffer, phase, d, owner, to):
        return pltpu.make_async_remote_copy(
            src_ref=src.at[to], dst_ref=buffer.at[owner], send_sem=y_send.at[phase, d],
            recv_sem=y_recv.at[phase, owner], device_id=(ix, to), device_id_type=MESH,
        )

    def y_start(src, buffer, phase):
        for d, other in y_others:
            y_copy(src, buffer, phase, d, iy, other).start()
        buffer[iy] = src[iy]

    def y_wait(src, buffer, phase):
        for d, other in y_others:
            y_copy(src, buffer, phase, d, other, other).wait_recv()

    def y_pack(buffer, plane, ref, at):
        for k in range(ny):
            buffer[k, plane * rows:(plane + 1) * rows, :] = ref[k * rows:(k + 1) * rows, at, :]

    at_x, at_y, at_z = (position(material.shape, axis) for axis in range(3))
    diagonal = excess + 2.0

    factor(jnp.where((at_y == 0) & (iy == 0), diagonal - 1.0, diagonal), 1, fy)
    vly[...] = apply(jnp.where(at_y == 0, 1.0, 0.0), 1, fy)
    vry[...] = apply(jnp.where(at_y == cy - 1, 1.0, 0.0), 1, fy)
    y_pack(ym_s, 0, vly, 0)
    y_pack(ym_s, 1, vry, 0)
    y_pack(ym_s, 2, vry, cy - 1)
    y_start(ym_s, ym_r, 0)
    factor(jnp.where((at_x == 0) & (ix == 0), diagonal - 1.0, diagonal), 0, fx)
    vlx[...] = apply(jnp.where(at_x == 0, 1.0, 0.0), 0, fx)
    vrx[...] = apply(jnp.where(at_x == cx - 1, 1.0, 0.0), 0, fx)
    xm_s[0] = vlx[0]
    xm_s[1] = vrx[0]
    xm_s[2] = vrx[cx - 1]
    x_start(xm_s, xm_r, 0)

    def forward_z(v):
        return jnp.where(at_z == cz - 1, 0.0, shift(v, -1, 2)) - v

    def backward_z(v):
        return v - jnp.where(at_z == 0, 0.0, shift(v, 1, 2))

    def forward_y(v, upper):
        return jnp.where(at_y == cy - 1, upper, shift(v, -1, 1)) - v

    def backward_y(v, lower):
        return v - jnp.where(at_y == 0, lower, shift(v, 1, 1))

    def forward_x(v, upper):
        return jnp.concatenate([v[1:], upper], axis=0) - v

    def backward_x(v, lower):
        return v - jnp.concatenate([lower, v[:-1]], axis=0)

    no_x = jnp.zeros((1, cy, cz), jnp.float32)
    scale = 1.0 / half_step

    def x_send_block(source, absorbed, sign, phase):
        w = apply(source, 0, fx)
        xa_s[phase - 1, 0] = w[0]
        xa_s[phase - 1, 1] = w[cx - 1] - sign * scale * absorbed[cx - 1]
        x_start(xa_s.at[phase - 1], xa_r.at[phase - 1], phase)
        return w

    def y_send_block(source, absorbed, sign, phase):
        w = apply(source, 1, fy)
        w_ref[phase - 1] = w
        pq_ref[...] = w - (sign * scale) * absorbed
        y_pack(ya_s.at[phase - 1], 0, w_ref.at[phase - 1], 0)
        y_pack(ya_s.at[phase - 1], 1, pq_ref, cy - 1)
        y_start(ya_s.at[phase - 1], ya_r.at[phase - 1], phase)

    def x_finish(w, phase, matrix):
        first, cross, terms = matrix
        x_wait(xa_s.at[phase - 1], xa_r.at[phase - 1], phase)
        p, q = sweep(
            first, cross, terms,
            [xa_r[phase - 1, k, 0] for k in range(nx)], [xa_r[phase - 1, k, 1] for k in range(nx)],
        )
        p_ref[0] = jnp.zeros_like(p[0])
        for k in range(nx):
            p_ref[k + 1] = p[k]
            q_ref[k] = q[k]
        q_ref[nx] = q[nx]
        left, right = p_ref[ix], q_ref[ix + 1]
        u = w + vlx[...] * left[None] + vrx[...] * right[None]
        return u, left[None], right[None]

    def y_reduce(phase, matrix):
        first, cross, terms = matrix
        buffer = ya_r.at[phase - 1]
        y_wait(ya_s.at[phase - 1], buffer, phase)
        p, q = sweep(
            first, cross, terms,
            [buffer[k, 0:rows, :] for k in range(ny)], [buffer[k, rows:2 * rows, :] for k in range(ny)],
        )
        out = yb_s.at[phase - 1]
        for k in range(ny):
            out[k, 0:rows, :] = p[k - 1] if k else jnp.zeros_like(p[0])
            out[k, rows:2 * rows, :] = q[k + 1]
        y_start(out, yb_r.at[phase - 1], phase + 2)

    def y_finish(phase):
        buffer = yb_r.at[phase - 1]
        y_wait(yb_s.at[phase - 1], buffer, phase + 2)
        for k in range(ny):
            pq_ref[k * rows:(k + 1) * rows, 0, :] = buffer[k, 0:rows, :]
            pq_ref[k * rows:(k + 1) * rows, 1, :] = buffer[k, rows:2 * rows, :]
        left, right = pq_ref[:, 0:1, :], pq_ref[:, 1:2, :]
        return w_ref[phase - 1] + vly[...] * left + vry[...] * right, left, right

    interim_y = h_ref[1] - half_step * forward_z(e_ref[0])
    for copy, _, receives in halos:
        pl.when(receives)(copy.wait_recv)
    pq_ref[:, 0, :] = halo_yr[0]
    pq_ref[:, 1, :] = halo_yr[1]
    ez_above, hx_below = pq_ref[:, 0:1, :], pq_ref[:, 1:2, :]
    interim_z = h_ref[2] - half_step * forward_x(e_ref[1], halo_xr[0:1])
    y_send_block(
        carry * e_ref[0] + scale * (backward_y(interim_z, 0.0) - backward_z(h_ref[1])),
        interim_z, 1.0, 1,
    )
    w_center_z = x_send_block(
        carry * e_ref[2] + scale * (backward_x(interim_y, no_x) - backward_y(h_ref[0], hx_below)),
        interim_y, 1.0, 1,
    )
    x_wait(xm_s, xm_r, 0)
    first_x = [xm_r[k, 0] for k in range(nx)]
    cross_x = [xm_r[k, 1] for k in range(nx)]
    matrix_x = (first_x, cross_x, sweep_matrix(first_x, cross_x, [xm_r[k, 2] for k in range(nx)]))
    y_wait(ym_s, ym_r, 0)
    first_y = [ym_r[k, 0:rows, :] for k in range(ny)]
    cross_y = [ym_r[k, rows:2 * rows, :] for k in range(ny)]
    last_y = [ym_r[k, 2 * rows:3 * rows, :] for k in range(ny)]
    matrix_y = (first_y, cross_y, sweep_matrix(first_y, cross_y, last_y))

    factor(jnp.where(at_z == 0, diagonal - 1.0, diagonal), 2, fz)
    interim_x = h_ref[0] - half_step * forward_y(e_ref[2], ez_above)
    center_y = apply(
        carry * e_ref[1] + scale * (backward_z(interim_x) - backward_x(h_ref[2], halo_xr[1:2])), 2, fz
    )
    curl_x = half_step * forward_z(center_y)
    middle_x = interim_x + curl_x
    second_x = middle_x + curl_x

    y_reduce(1, matrix_y)
    center_z, left, right = x_finish(w_center_z, 1, matrix_x)
    curl_y = half_step * forward_x(center_z, right)
    middle_y = interim_y + curl_y
    second_y = middle_y + curl_y
    middle_y_below = jnp.where(ix > 0, half_step * (center_z[0:1] - left), 0.0)
    y_send_block(
        carry * center_z + scale * (backward_x(middle_y, middle_y_below) - backward_y(second_x, 0.0)),
        second_x, -1.0, 2,
    )
    center_x, left, right = y_finish(1)
    curl_z = half_step * forward_y(center_x, right)
    middle_z = interim_z + curl_z
    second_z = middle_z + curl_z
    w_final_y = x_send_block(
        carry * center_y + scale * (backward_z(middle_x) - backward_x(second_z, no_x)),
        second_z, -1.0, 2,
    )
    middle_z_below = jnp.where(iy > 0, half_step * (center_x[:, 0:1, :] - left), 0.0)
    y_reduce(2, matrix_y)
    final_x = apply(
        carry * center_x + scale * (backward_y(middle_z, middle_z_below) - backward_z(second_y)), 2, fz
    )
    eo_ref[0] = final_x
    ho_ref[1] = second_y - half_step * forward_z(final_x)
    final_y, _, right = x_finish(w_final_y, 2, matrix_x)
    eo_ref[1] = final_y
    ho_ref[2] = second_z - half_step * forward_x(final_y, right)
    final_z, _, right = y_finish(2)
    eo_ref[2] = final_z
    ho_ref[0] = second_x - half_step * forward_y(final_z, right)

    for copy, sends, _ in halos:
        pl.when(sends)(copy.wait_send)
    for phase, src in enumerate([xm_s, xa_s.at[0], xa_s.at[1]]):
        for d, other in x_others:
            x_copy(src, xm_r if phase == 0 else xa_r.at[phase - 1], phase, d, ix, other).wait_send()
    for phase, (src, buffer) in enumerate([
        (ym_s, ym_r), (ya_s.at[0], ya_r.at[0]), (ya_s.at[1], ya_r.at[1]),
        (yb_s.at[0], yb_r.at[0]), (yb_s.at[1], yb_r.at[1]),
    ]):
        for d, other in y_others:
            y_copy(src, buffer, phase, d, iy, other).wait_send()


def per_device(nx, ny, electric, magnetic, material, permittivity, conductivity):
    cx, cy, cz = material.shape
    rows = cx // ny
    cell = (cx, cy, cz)
    count = [2 * len(strides(length)) + 1 for length in cell]
    vmem = pltpu.VMEM

    def f32(*shape):
        return vmem(shape, jnp.float32)

    dma = pltpu.SemaphoreType.DMA
    return pl.pallas_call(
        functools.partial(kernel, nx, ny),
        out_shape=(
            jax.ShapeDtypeStruct(electric.shape, jnp.float32),
            jax.ShapeDtypeStruct(magnetic.shape, jnp.float32),
        ),
        in_specs=[pl.BlockSpec(memory_space=pltpu.VMEM)] * 3
        + [pl.BlockSpec(memory_space=pltpu.SMEM)] * 2,
        out_specs=(pl.BlockSpec(memory_space=pltpu.VMEM),) * 2,
        scratch_shapes=[
            f32(count[0], *cell), f32(count[1], *cell), f32(count[2], *cell),
            f32(*cell), f32(*cell), f32(*cell), f32(*cell),
            f32(2, cy, cz), f32(2, cx, cz), f32(2, cy, cz), f32(2, cx, cz),
            f32(3, cy, cz), f32(nx, 3, cy, cz), f32(2, 2, cy, cz), f32(2, nx, 2, cy, cz),
            f32(ny, 3 * rows, cz), f32(ny, 3 * rows, cz),
            f32(2, ny, 2 * rows, cz), f32(2, ny, 2 * rows, cz),
            f32(2, ny, 2 * rows, cz), f32(2, ny, 2 * rows, cz),
            f32(nx + 1, cy, cz), f32(nx + 1, cy, cz), f32(*cell), f32(2, *cell),
            dma((4,)), dma((4,)), dma((3, nx)), dma((3, nx)), dma((5, ny)), dma((5, ny)),
        ],
        compiler_params=pltpu.CompilerParams(
            collective_id=0, has_side_effects=True, vmem_limit_bytes=48 * 1024 * 1024
        ),
    )(electric, magnetic, material, permittivity, conductivity)


def solution(mesh):
    nx, ny = mesh.shape["gx"], mesh.shape["gy"]
    return jax.shard_map(
        functools.partial(per_device, nx, ny),
        mesh=mesh,
        in_specs=(
            P(None, "gx", "gy", None),
            P(None, "gx", "gy", None),
            P("gx", "gy", None),
            P(),
            P(),
        ),
        out_specs=(P(None, "gx", "gy", None), P(None, "gx", "gy", None)),
        check_vma=False,
    )
```

```python
import functools

import jax
import jax.numpy as jnp
from jax import lax
from jax.experimental import pallas as pl
from jax.experimental.pallas import tpu as pltpu
from jax.sharding import PartitionSpec as P

half_step = 12.0
MESH = pl.DeviceIdType.MESH


def strides(length):
    found, stride = [], 1
    while stride < length:
        found.append(stride)
        stride *= 2
    return found


def roll(v, by, axis):
    return pltpu.roll(v, by % v.shape[axis], axis)


def position(shape, axis):
    return lax.broadcasted_iota(jnp.int32, shape, axis)


def reduce_matrix(diagonal, above):
    length, levels = diagonal.shape[0], []
    for stride in strides(length):
        inverse = 1.0 / diagonal
        below = roll(above, stride, 0)
        from_below = -below * roll(inverse, stride, 0)
        from_above = -above * roll(inverse, -stride, 0)
        levels.append((stride, from_below, from_above))
        diagonal = diagonal + from_below * below + from_above * above
        if 2 * stride < length:
            above = from_above * roll(above, -stride, 0)
    return levels, 1.0 / diagonal


def reduce_source(source, system):
    levels, inverse = system
    for stride, from_below, from_above in levels:
        source = source + from_below * roll(source, stride, 0) + from_above * roll(source, -stride, 0)
    return source * inverse


def eliminate(diagonals):
    pivots = [1.0 / diagonals[0]]
    for diagonal in diagonals[1:]:
        pivots.append(1.0 / (diagonal - pivots[-1]))
    return pivots


def back(rows, pivots):
    result = [rows[-1]]
    for row, pivot in zip(rows[-2::-1], pivots[-2::-1]):
        result.append(row + pivot * result[-1])
    return result[::-1]


def solve(rows, pivots):
    done = [rows[0] * pivots[0]]
    for row, pivot in zip(rows[1:], pivots[1:]):
        done.append((row + done[-1]) * pivot)
    return back(done, pivots)


def corners(pivots):
    done = [pivots[0]]
    for pivot in pivots[1:]:
        done.append(done[-1] * pivot)
    last = [pivots[-1]]
    for pivot in pivots[-2::-1]:
        last.append(last[-1] * pivot)
    return back(done, pivots), last[::-1]


def dot(left, right):
    terms = [a * b for a, b in zip(left, right)]
    while len(terms) > 1:
        terms = [sum(terms[i:i + 2][1:], terms[i]) for i in range(0, len(terms), 2)]
    return terms[0]


def sweep_matrix(first, cross, last):
    gain, pivots, mults, gains = jnp.zeros_like(first[0]), [], [], []
    for k in range(len(first)):
        pivot = 1.0 / (1.0 - first[k] * gain)
        mult = cross[k] * pivot
        pivots.append(pivot)
        mults.append(mult)
        gains.append(gain)
        gain = last[k] + mult * gain * cross[k]
    gains.append(gain)
    return pivots, mults, gains


def sweep(first, cross, matrix, w_first, w_last):
    pivots, mults, gains = matrix
    count = len(first)
    sums = [jnp.zeros_like(w_first[0])]
    for k in range(count):
        sums.append(w_last[k] + mults[k] * (sums[k] + gains[k] * w_first[k]))
    p, q = [None] * count, [None] * (count + 1)
    q[count] = jnp.zeros_like(w_first[0])
    for k in reversed(range(count)):
        p[k] = sums[k + 1] + gains[k + 1] * q[k + 1]
        q[k] = pivots[k] * (w_first[k] + first[k] * sums[k] + cross[k] * q[k + 1])
    return p, q


def kernel(
    nx, ny,
    e_in, h_in, mat_in, eps_in, sig_in, eo_ref, ho_ref,
    e_ref, h_ref, mat_ref, eps_ref, sig_ref,
    halo_xs, halo_ys, halo_xr, halo_yr,
    xm_s, xm_r, xa_s, xa_r, ym_s, ym_r, ya_s, ya_r, yb_s, yb_r,
    p_ref, q_ref, pq_ref, plane_ref, yt_ref, zt_ref,
    load, halo_send, halo_recv, x_send, x_recv, y_send, y_recv,
):
    cx, cy, cz = mat_ref.shape
    rows = cx // ny
    lanes = yt_ref.shape[2]
    ix, iy = lax.axis_index("gx"), lax.axis_index("gy")
    x_others = [lax.rem(ix + d, nx) for d in range(1, nx)]
    y_others = [lax.rem(iy + d, ny) for d in range(1, ny)]

    loads = [
        pltpu.make_async_copy(src, dst, load.at[k])
        for k, (src, dst) in enumerate(
            [(mat_in, mat_ref), (eps_in, eps_ref), (sig_in, sig_ref), (e_in, e_ref), (h_in, h_ref)]
        )
    ]
    for copy in loads:
        copy.start()
    halo_xr[...] = jnp.zeros_like(halo_xr)
    halo_yr[...] = jnp.zeros_like(halo_yr)
    barrier = pltpu.get_barrier_semaphore()
    for other in x_others:
        pl.semaphore_signal(barrier, inc=1, device_id=(other, iy), device_id_type=MESH)
    for other in y_others:
        pl.semaphore_signal(barrier, inc=1, device_id=(ix, other), device_id_type=MESH)
    for copy in loads:
        copy.wait()

    halo_xs[0] = e_ref[1, 0]
    halo_xs[1] = h_ref[2, cx - 1]
    halo_ys[0] = e_ref[2, :, 0, :]
    halo_ys[1] = h_ref[0, :, cy - 1, :]
    pl.semaphore_wait(barrier, nx + ny - 2)

    def halo(src, dst, k, to):
        return pltpu.make_async_remote_copy(
            src_ref=src, dst_ref=dst, send_sem=halo_send.at[k], recv_sem=halo_recv.at[k],
            device_id=to, device_id_type=MESH,
        )

    halos = [
        (halo(halo_xs.at[0], halo_xr.at[0], 0, (lax.rem(ix + nx - 1, nx), iy)), ix > 0, ix < nx - 1),
        (halo(halo_xs.at[1], halo_xr.at[1], 1, (lax.rem(ix + 1, nx), iy)), ix < nx - 1, ix > 0),
        (halo(halo_ys.at[0], halo_yr.at[0], 2, (ix, lax.rem(iy + ny - 1, ny))), iy > 0, iy < ny - 1),
        (halo(halo_ys.at[1], halo_yr.at[1], 3, (ix, lax.rem(iy + 1, ny))), iy < ny - 1, iy > 0),
    ]
    for copy, sends, _ in halos:
        pl.when(sends)(copy.start)

    material = mat_ref[...]
    excess = jnp.zeros(material.shape, jnp.float32)
    carry = jnp.zeros(material.shape, jnp.float32)
    for row in range(eps_ref.shape[0]):
        permit = eps_ref[row] * (1.0 / half_step)
        lossy = sig_ref[row] * 0.5
        chosen = material == row
        excess = jnp.where(chosen, (permit + lossy) * (1.0 / half_step), excess)
        carry = jnp.where(chosen, (permit - lossy) * (1.0 / half_step), carry)

    def x_copy(src, dst, phase, to):
        return pltpu.make_async_remote_copy(
            src_ref=src, dst_ref=dst, send_sem=x_send.at[phase], recv_sem=x_recv.at[phase],
            device_id=(to, iy), device_id_type=MESH,
        )

    def x_start(src, buffer, phase):
        for other in x_others:
            x_copy(src, buffer.at[ix], phase, other).start()
        buffer[ix] = src[...]

    def x_all(buffer, phase):
        part = buffer.at[pl.ds(0, nx - 1)]
        return x_copy(part, part, phase, x_others[0])

    def y_copy(src, dst, phase, to):
        return pltpu.make_async_remote_copy(
            src_ref=src, dst_ref=dst, send_sem=y_send.at[phase], recv_sem=y_recv.at[phase],
            device_id=(ix, to), device_id_type=MESH,
        )

    def y_start(src, buffer, phase):
        for other in y_others:
            y_copy(src.at[other], buffer.at[iy], phase, other).start()
        buffer[iy] = src[iy]

    def y_all(buffer, phase):
        part = buffer.at[pl.ds(0, ny - 1)]
        return y_copy(part, part, phase, y_others[0])

    def y_pack(buffer, planes):
        for i, plane in enumerate(planes):
            plane_ref[i] = plane
        for k in range(ny):
            for i in range(len(planes)):
                buffer[k, i * rows:(i + 1) * rows, :] = plane_ref[i, k * rows:(k + 1) * rows, :]

    def y_store(v):
        flat = v.reshape(cx * cy, cz)
        for half in range(cz // lanes):
            yt_ref[half] = flat[:, half * lanes:(half + 1) * lanes]

    def y_row(k):
        return jnp.concatenate(
            [yt_ref[half, pl.ds(k, cx, stride=cy), :] for half in range(cz // lanes)], axis=1
        )

    def y_rows(v):
        y_store(v)
        return [y_row(k) for k in range(cy)]

    def y_natural(planes):
        for k, plane in enumerate(planes):
            for half in range(cz // lanes):
                yt_ref[half, pl.ds(k, cx, stride=cy), :] = plane[:, half * lanes:(half + 1) * lanes]
        return jnp.concatenate(
            [yt_ref[half] for half in range(cz // lanes)], axis=1
        ).reshape(cx, cy, cz)

    at_y, at_z = position(material.shape, 1), position(material.shape, 2)
    diagonal = excess + 2.0

    diagonals = y_rows(diagonal)
    diagonals[0] = jnp.where(iy == 0, diagonals[0] - 1.0, diagonals[0])
    pivots_y = eliminate(diagonals)
    left_y, right_y = corners(pivots_y)
    y_pack(ym_s, [left_y[0], right_y[0], right_y[-1]])
    y_start(ym_s, ym_r, 0)
    diagonals = [diagonal[k] for k in range(cx)]
    diagonals[0] = jnp.where(ix == 0, diagonals[0] - 1.0, diagonals[0])
    pivots_x = eliminate(diagonals)
    left_x, right_x = corners(pivots_x)
    xm_s[0] = left_x[0]
    xm_s[1] = right_x[0]
    xm_s[2] = right_x[-1]
    x_start(xm_s, xm_r, 0)

    block = zt_ref.shape[0] // 16
    count = cz // block

    def z_rows(v):
        zt_ref[...] = v.reshape(cx * cy, cz).T
        return [zt_ref[pl.ds(k, count, stride=block), :] for k in range(block)]

    def z_solve(v):
        planes = z_rows(v)
        inner, edge = planes[:-1], planes[-1]
        edge = edge + dot(right_z, inner) + jnp.where(
            at_block == count - 1, 0.0, roll(dot(left_z, inner), -1, 0)
        )
        edge = reduce_source(edge, system_z)
        inner[0] = inner[0] + jnp.where(at_block == 0, 0.0, roll(edge, 1, 0))
        inner[-1] = inner[-1] + edge
        for k, plane in enumerate(solve(inner, pivots_z) + [edge]):
            zt_ref[pl.ds(k, count, stride=block), :] = plane
        return zt_ref[...].T.reshape(cx, cy, cz)

    def forward_z(v):
        return jnp.where(at_z == cz - 1, 0.0, roll(v, -1, 2)) - v

    def backward_z(v):
        return v - jnp.where(at_z == 0, 0.0, roll(v, 1, 2))

    def forward_y(v, upper):
        return jnp.where(at_y == cy - 1, upper, roll(v, -1, 1)) - v

    def backward_y(v, lower):
        return v - jnp.where(at_y == 0, lower, roll(v, 1, 1))

    def forward_x(v, upper):
        return jnp.concatenate([v[1:], upper], axis=0) - v

    def backward_x(v, lower):
        return v - jnp.concatenate([lower, v[:-1]], axis=0)

    no_x = jnp.zeros((1, cy, cz), jnp.float32)
    scale = 1.0 / half_step

    def x_send_block(source, absorbed, sign, phase):
        planes = [source[k] for k in range(cx)]
        xa_s[phase - 1, 0] = dot(left_x, planes)
        xa_s[phase - 1, 1] = dot(right_x, planes) - (sign * scale) * absorbed[cx - 1]
        x_start(xa_s.at[phase - 1], xa_r.at[phase - 1], phase)
        return planes

    def y_send_block(source, absorbed, sign, phase):
        y_store(absorbed)
        last = y_row(cy - 1)
        planes = y_rows(source)
        y_pack(
            ya_s.at[phase - 1], [dot(left_y, planes), dot(right_y, planes) - (sign * scale) * last]
        )
        y_start(ya_s.at[phase - 1], ya_r.at[phase - 1], phase)
        return planes

    def x_finish(planes, phase, matrix):
        first, cross, terms = matrix
        x_all(xa_r.at[phase - 1], phase).wait_recv()
        p, q = sweep(
            first, cross, terms,
            [xa_r[phase - 1, k, 0] for k in range(nx)], [xa_r[phase - 1, k, 1] for k in range(nx)],
        )
        p_ref[0] = jnp.zeros_like(p[0])
        for k in range(nx):
            p_ref[k + 1] = p[k]
            q_ref[k] = q[k]
        q_ref[nx] = q[nx]
        left, right = p_ref[ix], q_ref[ix + 1]
        planes = [planes[0] + left] + planes[1:-1] + [planes[-1] + right]
        return jnp.stack(solve(planes, pivots_x)), left[None], right[None]

    def y_reduce(phase, matrix):
        first, cross, terms = matrix
        buffer = ya_r.at[phase - 1]
        y_all(buffer, phase).wait_recv()
        p, q = sweep(
            first, cross, terms,
            [buffer[k, 0:rows, :] for k in range(ny)], [buffer[k, rows:2 * rows, :] for k in range(ny)],
        )
        out = yb_s.at[phase - 1]
        for k in range(ny):
            out[k, 0:rows, :] = p[k - 1] if k else jnp.zeros_like(p[0])
            out[k, rows:2 * rows, :] = q[k + 1]
        y_start(out, yb_r.at[phase - 1], phase + 2)

    def y_finish(planes, phase):
        buffer = yb_r.at[phase - 1]
        y_all(buffer, phase + 2).wait_recv()
        for k in range(ny):
            for i in range(2):
                plane_ref[i, k * rows:(k + 1) * rows, :] = buffer[k, i * rows:(i + 1) * rows, :]
        left, right = plane_ref[0], plane_ref[1]
        pq_ref[:, 0, :] = left
        pq_ref[:, 1, :] = right
        planes = [planes[0] + left] + planes[1:-1] + [planes[-1] + right]
        return y_natural(solve(planes, pivots_y)), pq_ref[:, 0:1, :], pq_ref[:, 1:2, :]

    interim_y = h_ref[1] - half_step * forward_z(e_ref[0])
    for copy, _, receives in halos:
        pl.when(receives)(copy.wait_recv)
    interim_z = h_ref[2] - half_step * forward_x(e_ref[1], halo_xr[0:1])
    rows_center_x = y_send_block(
        carry * e_ref[0] + scale * (backward_y(interim_z, 0.0) - backward_z(h_ref[1])),
        interim_z, 1.0, 1,
    )
    pq_ref[:, 0, :] = halo_yr[0]
    pq_ref[:, 1, :] = halo_yr[1]
    ez_above, hx_below = pq_ref[:, 0:1, :], pq_ref[:, 1:2, :]
    rows_center_z = x_send_block(
        carry * e_ref[2] + scale * (backward_x(interim_y, no_x) - backward_y(h_ref[0], hx_below)),
        interim_y, 1.0, 1,
    )
    y_all(ym_r, 0).wait_recv()
    first_y = [ym_r[k, 0:rows, :] for k in range(ny)]
    cross_y = [ym_r[k, rows:2 * rows, :] for k in range(ny)]
    last_y = [ym_r[k, 2 * rows:3 * rows, :] for k in range(ny)]
    matrix_y = (first_y, cross_y, sweep_matrix(first_y, cross_y, last_y))
    x_all(xm_r, 0).wait_recv()
    first_x = [xm_r[k, 0] for k in range(nx)]
    cross_x = [xm_r[k, 1] for k in range(nx)]
    matrix_x = (first_x, cross_x, sweep_matrix(first_x, cross_x, [xm_r[k, 2] for k in range(nx)]))

    diagonals = z_rows(jnp.where(at_z == 0, diagonal - 1.0, diagonal))
    at_block = position(diagonals[0].shape, 0)
    pivots_z = eliminate(diagonals[:-1])
    left_z, right_z = corners(pivots_z)
    inside = at_block < count - 1
    system_z = reduce_matrix(
        diagonals[-1] - right_z[-1] - jnp.where(inside, roll(left_z[0], -1, 0), 0.0),
        jnp.where(inside, -roll(right_z[0], -1, 0), 0.0),
    )
    interim_x = h_ref[0] - half_step * forward_y(e_ref[2], ez_above)
    center_y = z_solve(
        carry * e_ref[1] + scale * (backward_z(interim_x) - backward_x(h_ref[2], halo_xr[1:2]))
    )
    curl_x = half_step * forward_z(center_y)
    middle_x = interim_x + curl_x
    second_x = middle_x + curl_x

    y_reduce(1, matrix_y)
    center_z, left, right = x_finish(rows_center_z, 1, matrix_x)
    curl_y = half_step * forward_x(center_z, right)
    middle_y = interim_y + curl_y
    second_y = middle_y + curl_y
    middle_y_below = jnp.where(ix > 0, half_step * (center_z[0:1] - left), 0.0)
    rows_final_z = y_send_block(
        carry * center_z + scale * (backward_x(middle_y, middle_y_below) - backward_y(second_x, 0.0)),
        second_x, -1.0, 2,
    )
    center_x, left, right = y_finish(rows_center_x, 1)
    curl_z = half_step * forward_y(center_x, right)
    middle_z = interim_z + curl_z
    second_z = middle_z + curl_z
    rows_final_y = x_send_block(
        carry * center_y + scale * (backward_z(middle_x) - backward_x(second_z, no_x)),
        second_z, -1.0, 2,
    )
    middle_z_below = jnp.where(iy > 0, half_step * (center_x[:, 0:1, :] - left), 0.0)
    y_reduce(2, matrix_y)
    final_x = z_solve(
        carry * center_x + scale * (backward_y(middle_z, middle_z_below) - backward_z(second_y))
    )
    eo_ref[0] = final_x
    ho_ref[1] = second_y - half_step * forward_z(final_x)
    final_y, _, right = x_finish(rows_final_y, 2, matrix_x)
    eo_ref[1] = final_y
    ho_ref[2] = second_z - half_step * forward_x(final_y, right)
    final_z, _, right = y_finish(rows_final_z, 2)
    eo_ref[2] = final_z
    ho_ref[0] = second_x - half_step * forward_y(final_z, right)

    for copy, sends, _ in halos:
        pl.when(sends)(copy.wait_send)
    for phase, buffer in enumerate([xm_r, xa_r.at[0], xa_r.at[1]]):
        x_all(buffer, phase).wait_send()
    for phase, buffer in enumerate([ym_r, ya_r.at[0], ya_r.at[1], yb_r.at[0], yb_r.at[1]]):
        y_all(buffer, phase).wait_send()


def write_out(e_ref, h_ref, e_out, h_out, done):
    copies = [
        pltpu.make_async_copy(src.at[k], dst.at[k], done.at[i, k])
        for i, (src, dst) in enumerate([(e_ref, e_out), (h_ref, h_out)])
        for k in range(3)
    ]
    for copy in copies:
        copy.start()
    for copy in copies:
        copy.wait()


def per_device(nx, ny, electric, magnetic, material, permittivity, conductivity):
    cx, cy, cz = material.shape
    rows = cx // ny
    cell = (cx, cy, cz)
    vmem, smem = pltpu.VMEM, pltpu.SMEM
    in_hbm = pl.BlockSpec(memory_space=pltpu.HBM)
    in_vmem = pl.BlockSpec(memory_space=pltpu.VMEM)

    def f32(*shape):
        return vmem(shape, jnp.float32)

    dma = pltpu.SemaphoreType.DMA
    fields = (
        jax.ShapeDtypeStruct(electric.shape, jnp.float32),
        jax.ShapeDtypeStruct(magnetic.shape, jnp.float32),
    )
    advanced = pl.pallas_call(
        functools.partial(kernel, nx, ny),
        out_shape=fields,
        in_specs=[in_hbm] * 5,
        out_specs=(in_vmem,) * 2,
        scratch_shapes=[
            f32(3, *cell), f32(3, *cell), vmem(cell, jnp.int32),
            smem(permittivity.shape, jnp.float32), smem(conductivity.shape, jnp.float32),
            f32(2, cy, cz), f32(2, cx, cz), f32(2, cy, cz), f32(2, cx, cz),
            f32(3, cy, cz), f32(nx, 3, cy, cz), f32(2, 2, cy, cz), f32(2, nx, 2, cy, cz),
            f32(ny, 3 * rows, cz), f32(ny, 3 * rows, cz),
            f32(2, ny, 2 * rows, cz), f32(2, ny, 2 * rows, cz),
            f32(2, ny, 2 * rows, cz), f32(2, ny, 2 * rows, cz),
            f32(nx + 1, cy, cz), f32(nx + 1, cy, cz), f32(*cell), f32(3, cx, cz),
            f32(cz // 128, cx * cy, 128), f32(cz, cx * cy),
            dma((5,)), dma((4,)), dma((4,)), dma((3,)), dma((3,)), dma((5,)), dma((5,)),
        ],
        compiler_params=pltpu.CompilerParams(
            collective_id=0, has_side_effects=True, vmem_limit_bytes=48 * 1024 * 1024
        ),
    )(electric, magnetic, material, permittivity, conductivity)
    return pl.pallas_call(
        write_out,
        out_shape=fields,
        in_specs=[in_vmem] * 2,
        out_specs=(in_hbm,) * 2,
        scratch_shapes=[dma((2, 3))],
    )(*advanced)


def solution(mesh):
    nx, ny = mesh.shape["gx"], mesh.shape["gy"]
    return jax.shard_map(
        functools.partial(per_device, nx, ny),
        mesh=mesh,
        in_specs=(
            P(None, "gx", "gy", None),
            P(None, "gx", "gy", None),
            P("gx", "gy", None),
            P(),
            P(),
        ),
        out_specs=(P(None, "gx", "gy", None), P(None, "gx", "gy", None)),
        check_vma=False,
    )
```

```python
import functools

import jax
import jax.numpy as jnp
from jax import lax
from jax.experimental import pallas as pl
from jax.experimental.pallas import tpu as pltpu
from jax.sharding import PartitionSpec as P

half_step = 12.0
MESH = pl.DeviceIdType.MESH


def strides(length):
    found, stride = [], 1
    while stride < length:
        found.append(stride)
        stride *= 2
    return found


def roll(v, by, axis):
    return pltpu.roll(v, by % v.shape[axis], axis)


def position(shape, axis):
    return lax.broadcasted_iota(jnp.int32, shape, axis)


def reduce_matrix(diagonal, above):
    length, levels = diagonal.shape[0], []
    for stride in strides(length):
        inverse = 1.0 / diagonal
        below = roll(above, stride, 0)
        from_below = -below * roll(inverse, stride, 0)
        from_above = -above * roll(inverse, -stride, 0)
        levels.append((stride, from_below, from_above))
        diagonal = diagonal + from_below * below + from_above * above
        if 2 * stride < length:
            above = from_above * roll(above, -stride, 0)
    return levels, 1.0 / diagonal


def reduce_source(source, system):
    levels, inverse = system
    for stride, from_below, from_above in levels:
        source = source + from_below * roll(source, stride, 0) + from_above * roll(source, -stride, 0)
    return source * inverse


def eliminate(diagonals):
    pivots = [1.0 / diagonals[0]]
    for diagonal in diagonals[1:]:
        pivots.append(1.0 / (diagonal - pivots[-1]))
    return pivots


def back(rows, pivots):
    result = [rows[-1]]
    for row, pivot in zip(rows[-2::-1], pivots[-2::-1]):
        result.append(row + pivot * result[-1])
    return result[::-1]


def solve(rows, pivots):
    done = [rows[0] * pivots[0]]
    for row, pivot in zip(rows[1:], pivots[1:]):
        done.append((row + done[-1]) * pivot)
    return back(done, pivots)


def corners(pivots):
    done = [pivots[0]]
    for pivot in pivots[1:]:
        done.append(done[-1] * pivot)
    last = [pivots[-1]]
    for pivot in pivots[-2::-1]:
        last.append(last[-1] * pivot)
    return back(done, pivots), last[::-1]


def dot(left, right):
    terms = [a * b for a, b in zip(left, right)]
    while len(terms) > 1:
        terms = [sum(terms[i:i + 2][1:], terms[i]) for i in range(0, len(terms), 2)]
    return terms[0]


def sweep_matrix(first, cross, last):
    gain, pivots, mults, gains = jnp.zeros_like(first[0]), [], [], []
    for k in range(len(first)):
        pivot = 1.0 / (1.0 - first[k] * gain)
        mult = cross[k] * pivot
        pivots.append(pivot)
        mults.append(mult)
        gains.append(gain)
        gain = last[k] + mult * gain * cross[k]
    gains.append(gain)
    return pivots, mults, gains


def sweep(first, cross, matrix, w_first, w_last):
    pivots, mults, gains = matrix
    count = len(first)
    sums = [jnp.zeros_like(w_first[0])]
    for k in range(count):
        sums.append(w_last[k] + mults[k] * (sums[k] + gains[k] * w_first[k]))
    p, q = [None] * count, [None] * (count + 1)
    q[count] = jnp.zeros_like(w_first[0])
    for k in reversed(range(count)):
        p[k] = sums[k + 1] + gains[k + 1] * q[k + 1]
        q[k] = pivots[k] * (w_first[k] + first[k] * sums[k] + cross[k] * q[k + 1])
    return p, q


def kernel(
    nx, ny,
    e_in, h_in, mat_in, eps_in, sig_in, out,
    e_ref, h_ref, mat_ref, eps_ref, sig_ref,
    halo_xs, halo_ys, halo_xr, halo_yr,
    xm_s, xm_r, xa_s, xa_r, ym_s, ym_r, ya_s, ya_r, yb_s, yb_r,
    p_ref, q_ref, pq_ref, plane_ref, yt_ref, zt_ref, out_ref,
    load, store, halo_send, halo_recv, x_send, x_recv, y_send, y_recv,
):
    cx, cy, cz = mat_ref.shape
    rows = cx // ny
    lanes = yt_ref.shape[2]
    ix, iy = lax.axis_index("gx"), lax.axis_index("gy")
    x_others = [lax.rem(ix + d, nx) for d in range(1, nx)]
    y_others = [lax.rem(iy + d, ny) for d in range(1, ny)]

    loads = [
        pltpu.make_async_copy(src, dst, load.at[k])
        for k, (src, dst) in enumerate(
            [(mat_in, mat_ref), (eps_in, eps_ref), (sig_in, sig_ref), (e_in, e_ref), (h_in, h_ref)]
        )
    ]
    for copy in loads:
        copy.start()
    halo_xr[...] = jnp.zeros_like(halo_xr)
    halo_yr[...] = jnp.zeros_like(halo_yr)
    barrier = pltpu.get_barrier_semaphore()
    for other in x_others:
        pl.semaphore_signal(barrier, inc=1, device_id=(other, iy), device_id_type=MESH)
    for other in y_others:
        pl.semaphore_signal(barrier, inc=1, device_id=(ix, other), device_id_type=MESH)
    for copy in loads[:3]:
        copy.wait()
    material = mat_ref[...]
    excess = jnp.zeros(material.shape, jnp.float32)
    carry = jnp.zeros(material.shape, jnp.float32)
    for row in range(eps_ref.shape[0]):
        permit = eps_ref[row] * (1.0 / half_step)
        lossy = sig_ref[row] * 0.5
        chosen = material == row
        excess = jnp.where(chosen, (permit + lossy) * (1.0 / half_step), excess)
        carry = jnp.where(chosen, (permit - lossy) * (1.0 / half_step), carry)
    for copy in loads[3:]:
        copy.wait()

    halo_xs[0] = e_ref[1, 0]
    halo_xs[1] = h_ref[2, cx - 1]
    halo_ys[0] = e_ref[2, :, 0, :]
    halo_ys[1] = h_ref[0, :, cy - 1, :]
    pl.semaphore_wait(barrier, nx + ny - 2)

    def halo(src, dst, k, to):
        return pltpu.make_async_remote_copy(
            src_ref=src, dst_ref=dst, send_sem=halo_send.at[k], recv_sem=halo_recv.at[k],
            device_id=to, device_id_type=MESH,
        )

    halos = [
        (halo(halo_xs.at[0], halo_xr.at[0], 0, (lax.rem(ix + nx - 1, nx), iy)), ix > 0, ix < nx - 1),
        (halo(halo_xs.at[1], halo_xr.at[1], 1, (lax.rem(ix + 1, nx), iy)), ix < nx - 1, ix > 0),
        (halo(halo_ys.at[0], halo_yr.at[0], 2, (ix, lax.rem(iy + ny - 1, ny))), iy > 0, iy < ny - 1),
        (halo(halo_ys.at[1], halo_yr.at[1], 3, (ix, lax.rem(iy + 1, ny))), iy < ny - 1, iy > 0),
    ]
    for copy, sends, _ in halos:
        pl.when(sends)(copy.start)

    def emit(k, value):
        out_ref[k] = value
        pltpu.make_async_copy(out_ref.at[k], out.at[k], store.at[k]).start()

    def x_copy(src, dst, phase, to):
        return pltpu.make_async_remote_copy(
            src_ref=src, dst_ref=dst, send_sem=x_send.at[phase], recv_sem=x_recv.at[phase],
            device_id=(to, iy), device_id_type=MESH,
        )

    def x_start(src, buffer, phase):
        for other in x_others:
            x_copy(src, buffer.at[ix], phase, other).start()
        buffer[ix] = src[...]

    def x_all(buffer, phase):
        part = buffer.at[pl.ds(0, nx - 1)]
        return x_copy(part, part, phase, x_others[0])

    def y_copy(src, dst, phase, to):
        return pltpu.make_async_remote_copy(
            src_ref=src, dst_ref=dst, send_sem=y_send.at[phase], recv_sem=y_recv.at[phase],
            device_id=(ix, to), device_id_type=MESH,
        )

    def y_start(src, buffer, phase):
        for other in y_others:
            y_copy(src.at[other], buffer.at[iy], phase, other).start()
        buffer[iy] = src[iy]

    def y_all(buffer, phase):
        part = buffer.at[pl.ds(0, ny - 1)]
        return y_copy(part, part, phase, y_others[0])

    def y_pack(buffer, planes):
        for i, plane in enumerate(planes):
            plane_ref[i] = plane
        for k in range(ny):
            for i in range(len(planes)):
                buffer[k, i * rows:(i + 1) * rows, :] = plane_ref[i, k * rows:(k + 1) * rows, :]

    def y_store(v):
        flat = v.reshape(cx * cy, cz)
        for half in range(cz // lanes):
            yt_ref[half] = flat[:, half * lanes:(half + 1) * lanes]

    def y_row(k):
        return jnp.concatenate(
            [yt_ref[half, pl.ds(k, cx, stride=cy), :] for half in range(cz // lanes)], axis=1
        )

    def y_rows(v):
        y_store(v)
        return [y_row(k) for k in range(cy)]

    def y_natural(planes):
        for k, plane in enumerate(planes):
            for half in range(cz // lanes):
                yt_ref[half, pl.ds(k, cx, stride=cy), :] = plane[:, half * lanes:(half + 1) * lanes]
        return jnp.concatenate(
            [yt_ref[half] for half in range(cz // lanes)], axis=1
        ).reshape(cx, cy, cz)

    at_y, at_z = position(material.shape, 1), position(material.shape, 2)
    diagonal = excess + 2.0

    diagonals = y_rows(diagonal)
    diagonals[0] = jnp.where(iy == 0, diagonals[0] - 1.0, diagonals[0])
    pivots_y = eliminate(diagonals)
    left_y, right_y = corners(pivots_y)
    y_pack(ym_s, [left_y[0], right_y[0], right_y[-1]])
    y_start(ym_s, ym_r, 0)
    diagonals = [diagonal[k] for k in range(cx)]
    diagonals[0] = jnp.where(ix == 0, diagonals[0] - 1.0, diagonals[0])
    pivots_x = eliminate(diagonals)
    left_x, right_x = corners(pivots_x)
    xm_s[0] = left_x[0]
    xm_s[1] = right_x[0]
    xm_s[2] = right_x[-1]
    x_start(xm_s, xm_r, 0)

    block = zt_ref.shape[0] // 16
    count = cz // block

    def z_rows(v):
        zt_ref[...] = v.reshape(cx * cy, cz).T
        return [zt_ref[pl.ds(k, count, stride=block), :] for k in range(block)]

    def z_solve(v):
        planes = z_rows(v)
        inner, edge = planes[:-1], planes[-1]
        edge = edge + dot(right_z, inner) + jnp.where(
            at_block == count - 1, 0.0, roll(dot(left_z, inner), -1, 0)
        )
        edge = reduce_source(edge, system_z)
        inner[0] = inner[0] + jnp.where(at_block == 0, 0.0, roll(edge, 1, 0))
        inner[-1] = inner[-1] + edge
        for k, plane in enumerate(solve(inner, pivots_z) + [edge]):
            zt_ref[pl.ds(k, count, stride=block), :] = plane
        return zt_ref[...].T.reshape(cx, cy, cz)

    def forward_z(v):
        return jnp.where(at_z == cz - 1, 0.0, roll(v, -1, 2)) - v

    def backward_z(v):
        return v - jnp.where(at_z == 0, 0.0, roll(v, 1, 2))

    def forward_y(v, upper):
        return jnp.where(at_y == cy - 1, upper, roll(v, -1, 1)) - v

    def backward_y(v, lower):
        return v - jnp.where(at_y == 0, lower, roll(v, 1, 1))

    def forward_x(v, upper):
        return jnp.concatenate([v[1:], upper], axis=0) - v

    def backward_x(v, lower):
        return v - jnp.concatenate([lower, v[:-1]], axis=0)

    no_x = jnp.zeros((1, cy, cz), jnp.float32)
    scale = 1.0 / half_step

    def x_send_block(source, absorbed, sign, phase):
        planes = [source[k] for k in range(cx)]
        xa_s[phase - 1, 0] = dot(left_x, planes)
        xa_s[phase - 1, 1] = dot(right_x, planes) - (sign * scale) * absorbed[cx - 1]
        x_start(xa_s.at[phase - 1], xa_r.at[phase - 1], phase)
        return planes

    def y_send_block(source, absorbed, sign, phase):
        y_store(absorbed)
        last = y_row(cy - 1)
        planes = y_rows(source)
        y_pack(
            ya_s.at[phase - 1], [dot(left_y, planes), dot(right_y, planes) - (sign * scale) * last]
        )
        y_start(ya_s.at[phase - 1], ya_r.at[phase - 1], phase)
        return planes

    def x_finish(planes, phase, matrix):
        first, cross, terms = matrix
        x_all(xa_r.at[phase - 1], phase).wait_recv()
        p, q = sweep(
            first, cross, terms,
            [xa_r[phase - 1, k, 0] for k in range(nx)], [xa_r[phase - 1, k, 1] for k in range(nx)],
        )
        p_ref[0] = jnp.zeros_like(p[0])
        for k in range(nx):
            p_ref[k + 1] = p[k]
            q_ref[k] = q[k]
        q_ref[nx] = q[nx]
        left, right = p_ref[ix], q_ref[ix + 1]
        planes = [planes[0] + left] + planes[1:-1] + [planes[-1] + right]
        return jnp.stack(solve(planes, pivots_x)), left[None], right[None]

    def y_reduce(phase, matrix):
        first, cross, terms = matrix
        buffer = ya_r.at[phase - 1]
        y_all(buffer, phase).wait_recv()
        p, q = sweep(
            first, cross, terms,
            [buffer[k, 0:rows, :] for k in range(ny)], [buffer[k, rows:2 * rows, :] for k in range(ny)],
        )
        out = yb_s.at[phase - 1]
        for k in range(ny):
            out[k, 0:rows, :] = p[k - 1] if k else jnp.zeros_like(p[0])
            out[k, rows:2 * rows, :] = q[k + 1]
        y_start(out, yb_r.at[phase - 1], phase + 2)

    def y_finish(planes, phase):
        buffer = yb_r.at[phase - 1]
        y_all(buffer, phase + 2).wait_recv()
        for k in range(ny):
            for i in range(2):
                plane_ref[i, k * rows:(k + 1) * rows, :] = buffer[k, i * rows:(i + 1) * rows, :]
        left, right = plane_ref[0], plane_ref[1]
        pq_ref[:, 0, :] = left
        pq_ref[:, 1, :] = right
        planes = [planes[0] + left] + planes[1:-1] + [planes[-1] + right]
        return y_natural(solve(planes, pivots_y)), pq_ref[:, 0:1, :], pq_ref[:, 1:2, :]

    interim_y = h_ref[1] - half_step * forward_z(e_ref[0])
    for copy, _, receives in halos:
        pl.when(receives)(copy.wait_recv)
    interim_z = h_ref[2] - half_step * forward_x(e_ref[1], halo_xr[0:1])
    rows_center_x = y_send_block(
        carry * e_ref[0] + scale * (backward_y(interim_z, 0.0) - backward_z(h_ref[1])),
        interim_z, 1.0, 1,
    )
    pq_ref[:, 0, :] = halo_yr[0]
    pq_ref[:, 1, :] = halo_yr[1]
    ez_above, hx_below = pq_ref[:, 0:1, :], pq_ref[:, 1:2, :]
    rows_center_z = x_send_block(
        carry * e_ref[2] + scale * (backward_x(interim_y, no_x) - backward_y(h_ref[0], hx_below)),
        interim_y, 1.0, 1,
    )
    y_all(ym_r, 0).wait_recv()
    first_y = [ym_r[k, 0:rows, :] for k in range(ny)]
    cross_y = [ym_r[k, rows:2 * rows, :] for k in range(ny)]
    last_y = [ym_r[k, 2 * rows:3 * rows, :] for k in range(ny)]
    matrix_y = (first_y, cross_y, sweep_matrix(first_y, cross_y, last_y))
    x_all(xm_r, 0).wait_recv()
    first_x = [xm_r[k, 0] for k in range(nx)]
    cross_x = [xm_r[k, 1] for k in range(nx)]
    matrix_x = (first_x, cross_x, sweep_matrix(first_x, cross_x, [xm_r[k, 2] for k in range(nx)]))

    diagonals = z_rows(jnp.where(at_z == 0, diagonal - 1.0, diagonal))
    at_block = position(diagonals[0].shape, 0)
    pivots_z = eliminate(diagonals[:-1])
    left_z, right_z = corners(pivots_z)
    inside = at_block < count - 1
    system_z = reduce_matrix(
        diagonals[-1] - right_z[-1] - jnp.where(inside, roll(left_z[0], -1, 0), 0.0),
        jnp.where(inside, -roll(right_z[0], -1, 0), 0.0),
    )
    interim_x = h_ref[0] - half_step * forward_y(e_ref[2], ez_above)
    center_y = z_solve(
        carry * e_ref[1] + scale * (backward_z(interim_x) - backward_x(h_ref[2], halo_xr[1:2]))
    )
    curl_x = half_step * forward_z(center_y)
    middle_x = interim_x + curl_x
    second_x = middle_x + curl_x

    y_reduce(1, matrix_y)
    center_z, left, right = x_finish(rows_center_z, 1, matrix_x)
    curl_y = half_step * forward_x(center_z, right)
    middle_y = interim_y + curl_y
    second_y = middle_y + curl_y
    middle_y_below = jnp.where(ix > 0, half_step * (center_z[0:1] - left), 0.0)
    rows_final_z = y_send_block(
        carry * center_z + scale * (backward_x(middle_y, middle_y_below) - backward_y(second_x, 0.0)),
        second_x, -1.0, 2,
    )
    center_x, left, right = y_finish(rows_center_x, 1)
    curl_z = half_step * forward_y(center_x, right)
    middle_z = interim_z + curl_z
    second_z = middle_z + curl_z
    rows_final_y = x_send_block(
        carry * center_y + scale * (backward_z(middle_x) - backward_x(second_z, no_x)),
        second_z, -1.0, 2,
    )
    middle_z_below = jnp.where(iy > 0, half_step * (center_x[:, 0:1, :] - left), 0.0)
    y_reduce(2, matrix_y)
    final_x = z_solve(
        carry * center_x + scale * (backward_y(middle_z, middle_z_below) - backward_z(second_y))
    )
    emit(0, final_x)
    emit(4, second_y - half_step * forward_z(final_x))
    final_y, _, right = x_finish(rows_final_y, 2, matrix_x)
    emit(1, final_y)
    emit(5, second_z - half_step * forward_x(final_y, right))
    final_z, _, right = y_finish(rows_final_z, 2)
    emit(2, final_z)
    emit(3, second_x - half_step * forward_y(final_z, right))

    for k in range(6):
        pltpu.make_async_copy(out_ref.at[k], out.at[k], store.at[k]).wait()
    for copy, sends, _ in halos:
        pl.when(sends)(copy.wait_send)
    for phase, buffer in enumerate([xm_r, xa_r.at[0], xa_r.at[1]]):
        x_all(buffer, phase).wait_send()
    for phase, buffer in enumerate([ym_r, ya_r.at[0], ya_r.at[1], yb_r.at[0], yb_r.at[1]]):
        y_all(buffer, phase).wait_send()


def per_device(nx, ny, electric, magnetic, material, permittivity, conductivity):
    cx, cy, cz = material.shape
    rows = cx // ny
    cell = (cx, cy, cz)
    vmem, smem = pltpu.VMEM, pltpu.SMEM
    in_hbm = pl.BlockSpec(memory_space=pltpu.HBM)

    def f32(*shape):
        return vmem(shape, jnp.float32)

    dma = pltpu.SemaphoreType.DMA
    advanced = pl.pallas_call(
        functools.partial(kernel, nx, ny),
        out_shape=jax.ShapeDtypeStruct((6,) + cell, jnp.float32),
        in_specs=[in_hbm] * 5,
        out_specs=in_hbm,
        scratch_shapes=[
            f32(3, *cell), f32(3, *cell), vmem(cell, jnp.int32),
            smem(permittivity.shape, jnp.float32), smem(conductivity.shape, jnp.float32),
            f32(2, cy, cz), f32(2, cx, cz), f32(2, cy, cz), f32(2, cx, cz),
            f32(3, cy, cz), f32(nx, 3, cy, cz), f32(2, 2, cy, cz), f32(2, nx, 2, cy, cz),
            f32(ny, 3 * rows, cz), f32(ny, 3 * rows, cz),
            f32(2, ny, 2 * rows, cz), f32(2, ny, 2 * rows, cz),
            f32(2, ny, 2 * rows, cz), f32(2, ny, 2 * rows, cz),
            f32(nx + 1, cy, cz), f32(nx + 1, cy, cz), f32(*cell), f32(3, cx, cz),
            f32(cz // 128, cx * cy, 128), f32(cz, cx * cy), f32(6, *cell),
            dma((5,)), dma((6,)), dma((4,)), dma((4,)), dma((3,)), dma((3,)), dma((5,)), dma((5,)),
        ],
        compiler_params=pltpu.CompilerParams(
            collective_id=0, has_side_effects=True, vmem_limit_bytes=62 * 1024 * 1024
        ),
    )(electric, magnetic, material, permittivity, conductivity)
    return advanced[:3], advanced[3:]


def solution(mesh):
    nx, ny = mesh.shape["gx"], mesh.shape["gy"]
    return jax.shard_map(
        functools.partial(per_device, nx, ny),
        mesh=mesh,
        in_specs=(
            P(None, "gx", "gy", None),
            P(None, "gx", "gy", None),
            P("gx", "gy", None),
            P(),
            P(),
        ),
        out_specs=(P(None, "gx", "gy", None), P(None, "gx", "gy", None)),
        check_vma=False,
    )
```

```python
import functools

import jax
import jax.numpy as jnp
from jax import lax
from jax.experimental import pallas as pl
from jax.experimental.pallas import tpu as pltpu
from jax.sharding import PartitionSpec as P

half_step = 12.0
MESH = pl.DeviceIdType.MESH


def strides(length):
    found, stride = [], 1
    while stride < length:
        found.append(stride)
        stride *= 2
    return found


def roll(v, by, axis):
    return pltpu.roll(v, by % v.shape[axis], axis)


def position(shape, axis):
    return lax.broadcasted_iota(jnp.int32, shape, axis)


def reduce_matrix(diagonal, above):
    length, levels = diagonal.shape[0], []
    for stride in strides(length):
        inverse = 1.0 / diagonal
        below = roll(above, stride, 0)
        from_below = -below * roll(inverse, stride, 0)
        from_above = -above * roll(inverse, -stride, 0)
        levels.append((stride, from_below, from_above))
        diagonal = diagonal + from_below * below + from_above * above
        if 2 * stride < length:
            above = from_above * roll(above, -stride, 0)
    return levels, 1.0 / diagonal


def reduce_source(source, system):
    levels, inverse = system
    for stride, from_below, from_above in levels:
        source = source + from_below * roll(source, stride, 0) + from_above * roll(source, -stride, 0)
    return source * inverse


def eliminate(systems):
    found = [[1.0 / diagonals[0]] for diagonals in systems]
    for k in range(1, max(len(diagonals) for diagonals in systems)):
        for diagonals, pivots in zip(systems, found):
            if k < len(diagonals):
                pivots.append(1.0 / (diagonals[k] - pivots[-1]))
    return found


def back(rows, pivots):
    result = [rows[-1]]
    for row, pivot in zip(rows[-2::-1], pivots[-2::-1]):
        result.append(row + pivot * result[-1])
    return result[::-1]


def solve(rows, pivots):
    done = [rows[0] * pivots[0]]
    for row, pivot in zip(rows[1:], pivots[1:]):
        done.append((row + done[-1]) * pivot)
    return back(done, pivots)


def corners(pivots):
    done = [pivots[0]]
    for pivot in pivots[1:]:
        done.append(done[-1] * pivot)
    last = [pivots[-1]]
    for pivot in pivots[-2::-1]:
        last.append(last[-1] * pivot)
    return back(done, pivots), last[::-1]


def dot(left, right):
    terms = [a * b for a, b in zip(left, right)]
    while len(terms) > 1:
        terms = [sum(terms[i:i + 2][1:], terms[i]) for i in range(0, len(terms), 2)]
    return terms[0]


def sweep_matrix(first, cross, last):
    gain, pivots, mults, gains = jnp.zeros_like(first[0]), [], [], []
    for k in range(len(first)):
        pivot = 1.0 / (1.0 - first[k] * gain)
        mult = cross[k] * pivot
        pivots.append(pivot)
        mults.append(mult)
        gains.append(gain)
        gain = last[k] + mult * gain * cross[k]
    gains.append(gain)
    return pivots, mults, gains


def sweep(first, cross, matrix, w_first, w_last):
    pivots, mults, gains = matrix
    count = len(first)
    sums = [jnp.zeros_like(w_first[0])]
    for k in range(count):
        sums.append(w_last[k] + mults[k] * (sums[k] + gains[k] * w_first[k]))
    p, q = [None] * count, [None] * (count + 1)
    q[count] = jnp.zeros_like(w_first[0])
    for k in reversed(range(count)):
        p[k] = sums[k + 1] + gains[k + 1] * q[k + 1]
        q[k] = pivots[k] * (w_first[k] + first[k] * sums[k] + cross[k] * q[k + 1])
    return p, q


def solvers(ny):
    return (ny // 2, ny // 4) if ny % 4 == 0 else (ny, 0)


def kernel(
    nx, ny,
    e_in, h_in, mat_in, eps_in, sig_in, e_out, h_out,
    e_ref, h_ref, mat_ref, eps_ref, sig_ref,
    halo_xs, halo_ys, halo_xr, halo_yr,
    xm_s, xm_r, xa_s, xa_r, ym_s, ym_r, ya_s, ya_r, yb_s, yb_r, sweep_ref,
    p_ref, q_ref, pq_ref, plane_ref, yt_ref, zt_ref, out_ref,
    load, store, halo_send, halo_recv, x_send, x_recv, y_send, y_recv,
):
    cx, cy, cz = mat_ref.shape
    ns, s0 = solvers(ny)
    rows = cx // ns
    lanes = yt_ref.shape[2]
    ix, iy = lax.axis_index("gx"), lax.axis_index("gy")
    solving = (iy >= s0) & (iy < s0 + ns)
    x_others = [lax.rem(ix + d, nx) for d in range(1, nx)]
    y_others = [lax.rem(iy + d, ny) for d in range(1, ny)]

    loads = [
        pltpu.make_async_copy(src, dst, load.at[k])
        for k, (src, dst) in enumerate(
            [(mat_in, mat_ref), (eps_in, eps_ref), (sig_in, sig_ref), (e_in, e_ref), (h_in, h_ref)]
        )
    ]
    for copy in loads:
        copy.start()
    halo_xr[...] = jnp.zeros_like(halo_xr)
    halo_yr[...] = jnp.zeros_like(halo_yr)
    barrier = pltpu.get_barrier_semaphore()
    for other in x_others:
        pl.semaphore_signal(barrier, inc=1, device_id=(other, iy), device_id_type=MESH)
    for other in y_others:
        pl.semaphore_signal(barrier, inc=1, device_id=(ix, other), device_id_type=MESH)
    for copy in loads:
        copy.wait()

    halo_xs[0] = e_ref[1, 0]
    halo_xs[1] = h_ref[2, cx - 1]
    halo_ys[0] = e_ref[2, :, 0, :]
    halo_ys[1] = h_ref[0, :, cy - 1, :]
    pl.semaphore_wait(barrier, nx + ny - 2)

    def halo(src, dst, k, to):
        return pltpu.make_async_remote_copy(
            src_ref=src, dst_ref=dst, send_sem=halo_send.at[k], recv_sem=halo_recv.at[k],
            device_id=to, device_id_type=MESH,
        )

    halos = [
        (halo(halo_xs.at[0], halo_xr.at[0], 0, (lax.rem(ix + nx - 1, nx), iy)), ix > 0, ix < nx - 1),
        (halo(halo_xs.at[1], halo_xr.at[1], 1, (lax.rem(ix + 1, nx), iy)), ix < nx - 1, ix > 0),
        (halo(halo_ys.at[0], halo_yr.at[0], 2, (ix, lax.rem(iy + ny - 1, ny))), iy > 0, iy < ny - 1),
        (halo(halo_ys.at[1], halo_yr.at[1], 3, (ix, lax.rem(iy + 1, ny))), iy < ny - 1, iy > 0),
    ]
    for copy, sends, _ in halos:
        pl.when(sends)(copy.start)

    material = mat_ref[...]
    excess = jnp.zeros(material.shape, jnp.float32)
    carry = jnp.zeros(material.shape, jnp.float32)
    for row in range(eps_ref.shape[0]):
        permit = eps_ref[row] * (1.0 / half_step)
        lossy = sig_ref[row] * 0.5
        chosen = material == row
        excess = jnp.where(chosen, (permit + lossy) * (1.0 / half_step), excess)
        carry = jnp.where(chosen, (permit - lossy) * (1.0 / half_step), carry)

    out = [e_out.at[k] for k in range(3)] + [h_out.at[k] for k in range(3)]

    def emit(k, value):
        out_ref[k] = value
        pltpu.make_async_copy(out_ref.at[k], out[k], store.at[k]).start()

    def x_copy(src, dst, phase, to):
        return pltpu.make_async_remote_copy(
            src_ref=src, dst_ref=dst, send_sem=x_send.at[phase], recv_sem=x_recv.at[phase],
            device_id=(to, iy), device_id_type=MESH,
        )

    def x_start(src, buffer, phase):
        for other in x_others:
            x_copy(src, buffer.at[ix], phase, other).start()
        buffer[ix] = src[...]

    def x_all(buffer, phase):
        part = buffer.at[pl.ds(0, nx - 1)]
        return x_copy(part, part, phase, x_others[0])

    def y_copy(src, dst, phase, to):
        return pltpu.make_async_remote_copy(
            src_ref=src, dst_ref=dst, send_sem=y_send.at[phase], recv_sem=y_recv.at[phase],
            device_id=(ix, to), device_id_type=MESH,
        )

    def y_gather(src, buffer, phase):
        for d in range(ns):
            s = lax.rem(iy + d, ns)
            copy = y_copy(src.at[s], buffer.at[iy], phase, s0 + s)
            pl.when(iy != s0 + s)(copy.start)

        @pl.when(solving)
        def _():
            buffer[iy] = src[iy - s0]

    def y_scatter(src, buffer, phase):
        for other in y_others:
            y_copy(src.at[other], buffer.at[iy - s0], phase, other).start()
        buffer[iy - s0] = src[iy]

    def y_part(buffer, count, phase):
        part = buffer.at[pl.ds(0, count)]
        return y_copy(part, part, phase, y_others[0])

    def y_from_solvers(buffer, phase, send):
        for when, count in ((solving, ns - 1), (jnp.logical_not(solving), ns)):
            if count:
                copy = y_part(buffer, count, phase)
                pl.when(when)(copy.wait_send if send else copy.wait_recv)

    def y_pack(buffer, planes):
        for i, plane in enumerate(planes):
            plane_ref[i] = plane
        for k in range(ns):
            for i in range(len(planes)):
                buffer[k, i * rows:(i + 1) * rows, :] = plane_ref[i, k * rows:(k + 1) * rows, :]

    def y_store(v):
        flat = v.reshape(cx * cy, cz)
        for half in range(cz // lanes):
            yt_ref[half] = flat[:, half * lanes:(half + 1) * lanes]

    def y_row(k):
        return jnp.concatenate(
            [yt_ref[half, pl.ds(k, cx, stride=cy), :] for half in range(cz // lanes)], axis=1
        )

    def y_rows(v):
        y_store(v)
        return [y_row(k) for k in range(cy)]

    def y_natural(planes):
        for k, plane in enumerate(planes):
            for half in range(cz // lanes):
                yt_ref[half, pl.ds(k, cx, stride=cy), :] = plane[:, half * lanes:(half + 1) * lanes]
        return jnp.concatenate(
            [yt_ref[half] for half in range(cz // lanes)], axis=1
        ).reshape(cx, cy, cz)

    at_y, at_z = position(material.shape, 1), position(material.shape, 2)
    diagonal = excess + 2.0

    block = zt_ref.shape[0] // 16
    count = cz // block

    def z_rows(v):
        zt_ref[...] = v.reshape(cx * cy, cz).T
        return [zt_ref[pl.ds(k, count, stride=block), :] for k in range(block)]

    lines_x = [diagonal[k] for k in range(cx)]
    lines_x[0] = jnp.where(ix == 0, lines_x[0] - 1.0, lines_x[0])
    lines_y = y_rows(diagonal)
    lines_y[0] = jnp.where(iy == 0, lines_y[0] - 1.0, lines_y[0])
    lines_z = z_rows(jnp.where(at_z == 0, diagonal - 1.0, diagonal))
    pivots_x, pivots_y, pivots_z = eliminate([lines_x, lines_y, lines_z[:-1]])
    left_y, right_y = corners(pivots_y)
    left_x, right_x = corners(pivots_x)
    left_z, right_z = corners(pivots_z)
    y_pack(ym_s, [left_y[0], right_y[0], right_y[-1]])
    y_gather(ym_s, ym_r, 0)
    xm_s[0] = left_x[0]
    xm_s[1] = right_x[0]
    xm_s[2] = right_x[-1]
    x_start(xm_s, xm_r, 0)
    at_block = position(lines_z[0].shape, 0)
    inside = at_block < count - 1
    system_z = reduce_matrix(
        lines_z[-1] - right_z[-1] - jnp.where(inside, roll(left_z[0], -1, 0), 0.0),
        jnp.where(inside, -roll(right_z[0], -1, 0), 0.0),
    )

    def z_solve(v):
        planes = z_rows(v)
        inner, edge = planes[:-1], planes[-1]
        edge = edge + dot(right_z, inner) + jnp.where(
            at_block == count - 1, 0.0, roll(dot(left_z, inner), -1, 0)
        )
        edge = reduce_source(edge, system_z)
        inner[0] = inner[0] + jnp.where(at_block == 0, 0.0, roll(edge, 1, 0))
        inner[-1] = inner[-1] + edge
        for k, plane in enumerate(solve(inner, pivots_z) + [edge]):
            zt_ref[pl.ds(k, count, stride=block), :] = plane
        return zt_ref[...].T.reshape(cx, cy, cz)

    def forward_z(v):
        return jnp.where(at_z == cz - 1, 0.0, roll(v, -1, 2)) - v

    def backward_z(v):
        return v - jnp.where(at_z == 0, 0.0, roll(v, 1, 2))

    def forward_y(v, upper):
        return jnp.where(at_y == cy - 1, upper, roll(v, -1, 1)) - v

    def backward_y(v, lower):
        return v - jnp.where(at_y == 0, lower, roll(v, 1, 1))

    def forward_x(v, upper):
        return jnp.concatenate([v[1:], upper], axis=0) - v

    def backward_x(v, lower):
        return v - jnp.concatenate([lower, v[:-1]], axis=0)

    no_x = jnp.zeros((1, cy, cz), jnp.float32)
    scale = 1.0 / half_step

    def x_send_block(source, absorbed, sign, phase):
        planes = [source[k] for k in range(cx)]
        xa_s[phase - 1, 0] = dot(left_x, planes)
        xa_s[phase - 1, 1] = dot(right_x, planes) - (sign * scale) * absorbed[cx - 1]
        x_start(xa_s.at[phase - 1], xa_r.at[phase - 1], phase)
        return planes

    def y_send_block(source, absorbed, sign, phase):
        y_store(absorbed)
        last = y_row(cy - 1)
        planes = y_rows(source)
        y_pack(
            ya_s.at[phase - 1], [dot(left_y, planes), dot(right_y, planes) - (sign * scale) * last]
        )
        y_gather(ya_s.at[phase - 1], ya_r.at[phase - 1], phase)
        return planes

    def x_finish(planes, phase, matrix):
        first, cross, terms = matrix
        x_all(xa_r.at[phase - 1], phase).wait_recv()
        p, q = sweep(
            first, cross, terms,
            [xa_r[phase - 1, k, 0] for k in range(nx)], [xa_r[phase - 1, k, 1] for k in range(nx)],
        )
        p_ref[0] = jnp.zeros_like(p[0])
        for k in range(nx):
            p_ref[k + 1] = p[k]
            q_ref[k] = q[k]
        q_ref[nx] = q[nx]
        left, right = p_ref[ix], q_ref[ix + 1]
        planes = [planes[0] + left] + planes[1:-1] + [planes[-1] + right]
        return jnp.stack(solve(planes, pivots_x)), left[None], right[None]

    def y_reduce(phase):
        @pl.when(solving)
        def _():
            buffer = ya_r.at[phase - 1]
            y_part(buffer, ny - 1, phase).wait_recv()
            p, q = sweep(
                [ym_r[k, 0:rows, :] for k in range(ny)],
                [ym_r[k, rows:2 * rows, :] for k in range(ny)],
                [[sweep_ref[i, k] for k in range(ny + 1 if i == 2 else ny)] for i in range(3)],
                [buffer[k, 0:rows, :] for k in range(ny)],
                [buffer[k, rows:2 * rows, :] for k in range(ny)],
            )
            out = yb_s.at[phase - 1]
            for k in range(ny):
                out[k, 0:rows, :] = p[k - 1] if k else jnp.zeros_like(p[0])
                out[k, rows:2 * rows, :] = q[k + 1]
            y_scatter(out, yb_r.at[phase - 1], phase + 2)

    def y_finish(planes, phase):
        buffer = yb_r.at[phase - 1]
        y_from_solvers(buffer, phase + 2, False)
        for k in range(ns):
            for i in range(2):
                plane_ref[i, k * rows:(k + 1) * rows, :] = buffer[k, i * rows:(i + 1) * rows, :]
        left, right = plane_ref[0], plane_ref[1]
        pq_ref[:, 0, :] = left
        pq_ref[:, 1, :] = right
        planes = [planes[0] + left] + planes[1:-1] + [planes[-1] + right]
        return y_natural(solve(planes, pivots_y)), pq_ref[:, 0:1, :], pq_ref[:, 1:2, :]

    interim_y = h_ref[1] - half_step * forward_z(e_ref[0])
    for copy, _, receives in halos:
        pl.when(receives)(copy.wait_recv)
    interim_z = h_ref[2] - half_step * forward_x(e_ref[1], halo_xr[0:1])
    rows_center_x = y_send_block(
        carry * e_ref[0] + scale * (backward_y(interim_z, 0.0) - backward_z(h_ref[1])),
        interim_z, 1.0, 1,
    )
    pq_ref[:, 0, :] = halo_yr[0]
    pq_ref[:, 1, :] = halo_yr[1]
    ez_above, hx_below = pq_ref[:, 0:1, :], pq_ref[:, 1:2, :]
    rows_center_z = x_send_block(
        carry * e_ref[2] + scale * (backward_x(interim_y, no_x) - backward_y(h_ref[0], hx_below)),
        interim_y, 1.0, 1,
    )
    @pl.when(solving)
    def _():
        y_part(ym_r, ny - 1, 0).wait_recv()
        terms = sweep_matrix(
            *[[ym_r[k, i * rows:(i + 1) * rows, :] for k in range(ny)] for i in range(3)]
        )
        for i, planes in enumerate(terms):
            for k, plane in enumerate(planes):
                sweep_ref[i, k] = plane

    x_all(xm_r, 0).wait_recv()
    first_x = [xm_r[k, 0] for k in range(nx)]
    cross_x = [xm_r[k, 1] for k in range(nx)]
    matrix_x = (first_x, cross_x, sweep_matrix(first_x, cross_x, [xm_r[k, 2] for k in range(nx)]))

    interim_x = h_ref[0] - half_step * forward_y(e_ref[2], ez_above)
    center_y = z_solve(
        carry * e_ref[1] + scale * (backward_z(interim_x) - backward_x(h_ref[2], halo_xr[1:2]))
    )
    curl_x = half_step * forward_z(center_y)
    middle_x = interim_x + curl_x
    second_x = middle_x + curl_x

    y_reduce(1)
    center_z, left, right = x_finish(rows_center_z, 1, matrix_x)
    curl_y = half_step * forward_x(center_z, right)
    middle_y = interim_y + curl_y
    second_y = middle_y + curl_y
    middle_y_below = jnp.where(ix > 0, half_step * (center_z[0:1] - left), 0.0)
    rows_final_z = y_send_block(
        carry * center_z + scale * (backward_x(middle_y, middle_y_below) - backward_y(second_x, 0.0)),
        second_x, -1.0, 2,
    )
    center_x, left, right = y_finish(rows_center_x, 1)
    curl_z = half_step * forward_y(center_x, right)
    middle_z = interim_z + curl_z
    second_z = middle_z + curl_z
    rows_final_y = x_send_block(
        carry * center_y + scale * (backward_z(middle_x) - backward_x(second_z, no_x)),
        second_z, -1.0, 2,
    )
    middle_z_below = jnp.where(iy > 0, half_step * (center_x[:, 0:1, :] - left), 0.0)
    y_reduce(2)
    final_x = z_solve(
        carry * center_x + scale * (backward_y(middle_z, middle_z_below) - backward_z(second_y))
    )
    emit(0, final_x)
    emit(4, second_y - half_step * forward_z(final_x))
    final_y, _, right = x_finish(rows_final_y, 2, matrix_x)
    emit(1, final_y)
    emit(5, second_z - half_step * forward_x(final_y, right))
    final_z, _, right = y_finish(rows_final_z, 2)
    emit(2, final_z)
    emit(3, second_x - half_step * forward_y(final_z, right))

    for k in range(6):
        pltpu.make_async_copy(out_ref.at[k], out[k], store.at[k]).wait()
    for copy, sends, _ in halos:
        pl.when(sends)(copy.wait_send)
    for phase, buffer in enumerate([xm_r, xa_r.at[0], xa_r.at[1]]):
        x_all(buffer, phase).wait_send()
    for phase, buffer in enumerate([ym_s, ya_s.at[0], ya_s.at[1]]):
        y_from_solvers(buffer, phase, True)

    @pl.when(solving)
    def _():
        for phase in (3, 4):
            y_part(yb_s.at[phase - 3], ny - 1, phase).wait_send()


def per_device(nx, ny, electric, magnetic, material, permittivity, conductivity):
    cx, cy, cz = material.shape
    ns, _ = solvers(ny)
    rows = cx // ns
    cell = (cx, cy, cz)
    vmem, smem = pltpu.VMEM, pltpu.SMEM
    in_hbm = pl.BlockSpec(memory_space=pltpu.HBM)

    def f32(*shape):
        return vmem(shape, jnp.float32)

    dma = pltpu.SemaphoreType.DMA
    advanced = pl.pallas_call(
        functools.partial(kernel, nx, ny),
        out_shape=(jax.ShapeDtypeStruct((3,) + cell, jnp.float32),) * 2,
        in_specs=[in_hbm] * 5,
        out_specs=(in_hbm,) * 2,
        scratch_shapes=[
            f32(3, *cell), f32(3, *cell), vmem(cell, jnp.int32),
            smem(permittivity.shape, jnp.float32), smem(conductivity.shape, jnp.float32),
            f32(2, cy, cz), f32(2, cx, cz), f32(2, cy, cz), f32(2, cx, cz),
            f32(3, cy, cz), f32(nx, 3, cy, cz), f32(2, 2, cy, cz), f32(2, nx, 2, cy, cz),
            f32(ns, 3 * rows, cz), f32(ny, 3 * rows, cz),
            f32(2, ns, 2 * rows, cz), f32(2, ny, 2 * rows, cz),
            f32(2, ny, 2 * rows, cz), f32(2, ns, 2 * rows, cz), f32(3, ny + 1, rows, cz),
            f32(nx + 1, cy, cz), f32(nx + 1, cy, cz), f32(*cell), f32(3, cx, cz),
            f32(cz // 128, cx * cy, 128), f32(cz, cx * cy), f32(6, *cell),
            dma((5,)), dma((6,)), dma((4,)), dma((4,)), dma((3,)), dma((3,)), dma((5,)), dma((5,)),
        ],
        compiler_params=pltpu.CompilerParams(
            collective_id=0, has_side_effects=True, vmem_limit_bytes=62 * 1024 * 1024
        ),
    )(electric, magnetic, material, permittivity, conductivity)
    return advanced


def solution(mesh):
    nx, ny = mesh.shape["gx"], mesh.shape["gy"]
    return jax.shard_map(
        functools.partial(per_device, nx, ny),
        mesh=mesh,
        in_specs=(
            P(None, "gx", "gy", None),
            P(None, "gx", "gy", None),
            P("gx", "gy", None),
            P(),
            P(),
        ),
        out_specs=(P(None, "gx", "gy", None), P(None, "gx", "gy", None)),
        check_vma=False,
    )
```

```python
import functools

import jax
import jax.numpy as jnp
from jax import lax
from jax.experimental import pallas as pl
from jax.experimental.pallas import tpu as pltpu
from jax.sharding import PartitionSpec as P

half_step = 12.0
MESH = pl.DeviceIdType.MESH


def strides(length):
    found, stride = [], 1
    while stride < length:
        found.append(stride)
        stride *= 2
    return found


def roll(v, by, axis):
    return pltpu.roll(v, by % v.shape[axis], axis)


def position(shape, axis):
    return lax.broadcasted_iota(jnp.int32, shape, axis)


def reduce_matrix(diagonal, above):
    length, levels = diagonal.shape[0], []
    for stride in strides(length):
        inverse = 1.0 / diagonal
        below = roll(above, stride, 0)
        from_below = -below * roll(inverse, stride, 0)
        from_above = -above * roll(inverse, -stride, 0)
        levels.append((stride, from_below, from_above))
        diagonal = diagonal + from_below * below + from_above * above
        if 2 * stride < length:
            above = from_above * roll(above, -stride, 0)
    return levels, 1.0 / diagonal


def reduce_source(source, system):
    levels, inverse = system
    for stride, from_below, from_above in levels:
        source = source + from_below * roll(source, stride, 0) + from_above * roll(source, -stride, 0)
    return source * inverse


def eliminate(systems):
    found = [[1.0 / diagonals[0]] for diagonals in systems]
    for k in range(1, max(len(diagonals) for diagonals in systems)):
        for diagonals, pivots in zip(systems, found):
            if k < len(diagonals):
                pivots.append(1.0 / (diagonals[k] - pivots[-1]))
    return found


def back(rows, pivots):
    result = [rows[-1]]
    for row, pivot in zip(rows[-2::-1], pivots[-2::-1]):
        result.append(row + pivot * result[-1])
    return result[::-1]


def solve(rows, pivots):
    done = [rows[0] * pivots[0]]
    for row, pivot in zip(rows[1:], pivots[1:]):
        done.append((row + done[-1]) * pivot)
    return back(done, pivots)


def corners(pivots):
    done = [pivots[0]]
    for pivot in pivots[1:]:
        done.append(done[-1] * pivot)
    last = [pivots[-1]]
    for pivot in pivots[-2::-1]:
        last.append(last[-1] * pivot)
    return back(done, pivots), last[::-1]


def dot(left, right):
    terms = [a * b for a, b in zip(left, right)]
    while len(terms) > 1:
        terms = [sum(terms[i:i + 2][1:], terms[i]) for i in range(0, len(terms), 2)]
    return terms[0]


def sweep_matrix(first, cross, last):
    gain, pivots, mults, gains = jnp.zeros_like(first[0]), [], [], []
    for k in range(len(first)):
        pivot = 1.0 / (1.0 - first[k] * gain)
        mult = cross[k] * pivot
        pivots.append(pivot)
        mults.append(mult)
        gains.append(gain)
        gain = last[k] + mult * gain * cross[k]
    gains.append(gain)
    return pivots, mults, gains


def sweep(first, cross, matrix, w_first, w_last):
    pivots, mults, gains = matrix
    count = len(first)
    sums = [jnp.zeros_like(w_first[0])]
    for k in range(count):
        sums.append(w_last[k] + mults[k] * (sums[k] + gains[k] * w_first[k]))
    p, q = [None] * count, [None] * (count + 1)
    q[count] = jnp.zeros_like(w_first[0])
    for k in reversed(range(count)):
        p[k] = sums[k + 1] + gains[k + 1] * q[k + 1]
        q[k] = pivots[k] * (w_first[k] + first[k] * sums[k] + cross[k] * q[k + 1])
    return p, q


def solvers(ny):
    return (ny // 2, ny // 4) if ny % 4 == 0 else (ny, 0)


def kernel(
    nx, ny,
    e_in, h_in, mat_in, eps_in, sig_in, e_out, h_out,
    e_ref, h_ref, mat_ref, eps_ref, sig_ref,
    halo_xr, halo_yr,
    xm_s, xm_r, xa_s, xa_r, ym_s, ym_r, ya_s, ya_r, yb_s, yb_r, sweep_ref,
    p_ref, q_ref, pq_ref, plane_ref, yt_ref, zt_ref, out_ref,
    load, store, halo_send, halo_recv, x_send, x_recv, y_send, y_recv,
):
    cx, cy, cz = mat_ref.shape
    ns, s0 = solvers(ny)
    rows = cx // ns
    lanes = yt_ref.shape[2]
    ix, iy = lax.axis_index("gx"), lax.axis_index("gy")
    solving = (iy >= s0) & (iy < s0 + ns)
    x_others = [lax.rem(ix + d, nx) for d in range(1, nx)]
    y_others = [lax.rem(iy + d, ny) for d in range(1, ny)]

    loads = [
        pltpu.make_async_copy(src, dst, load.at[k])
        for k, (src, dst) in enumerate(
            [(mat_in, mat_ref), (eps_in, eps_ref), (sig_in, sig_ref), (e_in, e_ref), (h_in, h_ref)]
        )
    ]
    for copy in loads:
        copy.start()
    halo_xr[...] = jnp.zeros_like(halo_xr)
    halo_yr[...] = jnp.zeros_like(halo_yr)
    barrier = pltpu.get_barrier_semaphore()
    for other in x_others:
        pl.semaphore_signal(barrier, inc=1, device_id=(other, iy), device_id_type=MESH)
    for other in y_others:
        pl.semaphore_signal(barrier, inc=1, device_id=(ix, other), device_id_type=MESH)
    pl.semaphore_wait(barrier, nx + ny - 2)

    def halo(src, dst, k, to):
        return pltpu.make_async_remote_copy(
            src_ref=src, dst_ref=dst, send_sem=halo_send.at[k], recv_sem=halo_recv.at[k],
            device_id=to, device_id_type=MESH,
        )

    halos = [
        (halo(e_in.at[1, 0], halo_xr.at[0], 0, (lax.rem(ix + nx - 1, nx), iy)), ix > 0, ix < nx - 1),
        (halo(h_in.at[2, cx - 1], halo_xr.at[1], 1, (lax.rem(ix + 1, nx), iy)), ix < nx - 1, ix > 0),
        (halo(e_in.at[2, :, 0], halo_yr.at[0], 2, (ix, lax.rem(iy + ny - 1, ny))), iy > 0, iy < ny - 1),
        (halo(h_in.at[0, :, cy - 1], halo_yr.at[1], 3, (ix, lax.rem(iy + 1, ny))), iy < ny - 1, iy > 0),
    ]
    for copy, sends, _ in halos:
        pl.when(sends)(copy.start)
    for copy in loads[:3]:
        copy.wait()

    material = mat_ref[...]
    excess = jnp.zeros(material.shape, jnp.float32)
    carry = jnp.zeros(material.shape, jnp.float32)
    for row in range(eps_ref.shape[0]):
        permit = eps_ref[row] * (1.0 / half_step)
        lossy = sig_ref[row] * 0.5
        chosen = material == row
        excess = jnp.where(chosen, (permit + lossy) * (1.0 / half_step), excess)
        carry = jnp.where(chosen, (permit - lossy) * (1.0 / half_step), carry)

    out = [e_out.at[k] for k in range(3)] + [h_out.at[k] for k in range(3)]

    def emit(k, value):
        out_ref[k] = value
        pltpu.make_async_copy(out_ref.at[k], out[k], store.at[k]).start()

    def x_copy(src, dst, phase, to):
        return pltpu.make_async_remote_copy(
            src_ref=src, dst_ref=dst, send_sem=x_send.at[phase], recv_sem=x_recv.at[phase],
            device_id=(to, iy), device_id_type=MESH,
        )

    def x_start(src, buffer, phase):
        for other in x_others:
            x_copy(src, buffer.at[ix], phase, other).start()
        buffer[ix] = src[...]

    def x_all(buffer, phase):
        part = buffer.at[pl.ds(0, nx - 1)]
        return x_copy(part, part, phase, x_others[0])

    def y_copy(src, dst, phase, to):
        return pltpu.make_async_remote_copy(
            src_ref=src, dst_ref=dst, send_sem=y_send.at[phase], recv_sem=y_recv.at[phase],
            device_id=(ix, to), device_id_type=MESH,
        )

    def y_gather(src, buffer, phase):
        for d in range(ns):
            s = lax.rem(iy + d, ns)
            copy = y_copy(src.at[s], buffer.at[iy], phase, s0 + s)
            pl.when(iy != s0 + s)(copy.start)

        @pl.when(solving)
        def _():
            buffer[iy] = src[iy - s0]

    def y_scatter(src, buffer, phase):
        for other in y_others:
            y_copy(src.at[other], buffer.at[iy - s0], phase, other).start()
        buffer[iy - s0] = src[iy]

    def y_part(buffer, count, phase):
        part = buffer.at[pl.ds(0, count)]
        return y_copy(part, part, phase, y_others[0])

    def y_from_solvers(buffer, phase, send):
        for when, count in ((solving, ns - 1), (jnp.logical_not(solving), ns)):
            if count:
                copy = y_part(buffer, count, phase)
                pl.when(when)(copy.wait_send if send else copy.wait_recv)

    def y_pack(buffer, planes):
        for i, plane in enumerate(planes):
            plane_ref[i] = plane
        for k in range(ns):
            for i in range(len(planes)):
                buffer[k, i * rows:(i + 1) * rows, :] = plane_ref[i, k * rows:(k + 1) * rows, :]

    def y_store(v):
        flat = v.reshape(cx * cy, cz)
        for half in range(cz // lanes):
            yt_ref[half] = flat[:, half * lanes:(half + 1) * lanes]

    def y_row(k):
        return jnp.concatenate(
            [yt_ref[half, pl.ds(k, cx, stride=cy), :] for half in range(cz // lanes)], axis=1
        )

    def y_rows(v):
        y_store(v)
        return [y_row(k) for k in range(cy)]

    def y_natural(planes):
        for k, plane in enumerate(planes):
            for half in range(cz // lanes):
                yt_ref[half, pl.ds(k, cx, stride=cy), :] = plane[:, half * lanes:(half + 1) * lanes]
        return jnp.concatenate(
            [yt_ref[half] for half in range(cz // lanes)], axis=1
        ).reshape(cx, cy, cz)

    at_y, at_z = position(material.shape, 1), position(material.shape, 2)
    diagonal = excess + 2.0

    block = zt_ref.shape[0] // 16
    count = cz // block

    def z_rows(v):
        zt_ref[...] = v.reshape(cx * cy, cz).T
        return [zt_ref[pl.ds(k, count, stride=block), :] for k in range(block)]

    lines_x = [diagonal[k] for k in range(cx)]
    lines_x[0] = jnp.where(ix == 0, lines_x[0] - 1.0, lines_x[0])
    lines_y = y_rows(diagonal)
    lines_y[0] = jnp.where(iy == 0, lines_y[0] - 1.0, lines_y[0])
    lines_z = z_rows(jnp.where(at_z == 0, diagonal - 1.0, diagonal))
    pivots_x, pivots_y, pivots_z = eliminate([lines_x, lines_y, lines_z[:-1]])
    left_y, right_y = corners(pivots_y)
    left_x, right_x = corners(pivots_x)
    left_z, right_z = corners(pivots_z)
    y_pack(ym_s, [left_y[0], right_y[0], right_y[-1]])
    y_gather(ym_s, ym_r, 0)
    xm_s[0] = left_x[0]
    xm_s[1] = right_x[0]
    xm_s[2] = right_x[-1]
    x_start(xm_s, xm_r, 0)
    at_block = position(lines_z[0].shape, 0)
    inside = at_block < count - 1
    system_z = reduce_matrix(
        lines_z[-1] - right_z[-1] - jnp.where(inside, roll(left_z[0], -1, 0), 0.0),
        jnp.where(inside, -roll(right_z[0], -1, 0), 0.0),
    )

    def z_solve(v):
        planes = z_rows(v)
        inner, edge = planes[:-1], planes[-1]
        edge = edge + dot(right_z, inner) + jnp.where(
            at_block == count - 1, 0.0, roll(dot(left_z, inner), -1, 0)
        )
        edge = reduce_source(edge, system_z)
        inner[0] = inner[0] + jnp.where(at_block == 0, 0.0, roll(edge, 1, 0))
        inner[-1] = inner[-1] + edge
        for k, plane in enumerate(solve(inner, pivots_z) + [edge]):
            zt_ref[pl.ds(k, count, stride=block), :] = plane
        return zt_ref[...].T.reshape(cx, cy, cz)

    def forward_z(v):
        return jnp.where(at_z == cz - 1, 0.0, roll(v, -1, 2)) - v

    def backward_z(v):
        return v - jnp.where(at_z == 0, 0.0, roll(v, 1, 2))

    def forward_y(v, upper):
        return jnp.where(at_y == cy - 1, upper, roll(v, -1, 1)) - v

    def backward_y(v, lower):
        return v - jnp.where(at_y == 0, lower, roll(v, 1, 1))

    def forward_x(v, upper):
        return jnp.concatenate([v[1:], upper], axis=0) - v

    def backward_x(v, lower):
        return v - jnp.concatenate([lower, v[:-1]], axis=0)

    no_x = jnp.zeros((1, cy, cz), jnp.float32)
    scale = 1.0 / half_step

    def x_send_block(source, absorbed, sign, phase):
        planes = [source[k] for k in range(cx)]
        xa_s[phase - 1, 0] = dot(left_x, planes)
        xa_s[phase - 1, 1] = dot(right_x, planes) - (sign * scale) * absorbed[cx - 1]
        x_start(xa_s.at[phase - 1], xa_r.at[phase - 1], phase)
        return planes

    def y_send_block(source, absorbed, sign, phase):
        y_store(absorbed)
        last = y_row(cy - 1)
        planes = y_rows(source)
        y_pack(
            ya_s.at[phase - 1], [dot(left_y, planes), dot(right_y, planes) - (sign * scale) * last]
        )
        y_gather(ya_s.at[phase - 1], ya_r.at[phase - 1], phase)
        return planes

    def x_finish(planes, phase, matrix):
        first, cross, terms = matrix
        x_all(xa_r.at[phase - 1], phase).wait_recv()
        p, q = sweep(
            first, cross, terms,
            [xa_r[phase - 1, k, 0] for k in range(nx)], [xa_r[phase - 1, k, 1] for k in range(nx)],
        )
        p_ref[0] = jnp.zeros_like(p[0])
        for k in range(nx):
            p_ref[k + 1] = p[k]
            q_ref[k] = q[k]
        q_ref[nx] = q[nx]
        left, right = p_ref[ix], q_ref[ix + 1]
        planes = [planes[0] + left] + planes[1:-1] + [planes[-1] + right]
        return jnp.stack(solve(planes, pivots_x)), left[None], right[None]

    def y_reduce(phase):
        @pl.when(solving)
        def _():
            buffer = ya_r.at[phase - 1]
            y_part(buffer, ny - 1, phase).wait_recv()
            p, q = sweep(
                [ym_r[k, 0:rows, :] for k in range(ny)],
                [ym_r[k, rows:2 * rows, :] for k in range(ny)],
                [[sweep_ref[i, k] for k in range(ny + 1 if i == 2 else ny)] for i in range(3)],
                [buffer[k, 0:rows, :] for k in range(ny)],
                [buffer[k, rows:2 * rows, :] for k in range(ny)],
            )
            out = yb_s.at[phase - 1]
            for k in range(ny):
                out[k, 0:rows, :] = p[k - 1] if k else jnp.zeros_like(p[0])
                out[k, rows:2 * rows, :] = q[k + 1]
            y_scatter(out, yb_r.at[phase - 1], phase + 2)

    def y_finish(planes, phase):
        buffer = yb_r.at[phase - 1]
        y_from_solvers(buffer, phase + 2, False)
        for k in range(ns):
            for i in range(2):
                plane_ref[i, k * rows:(k + 1) * rows, :] = buffer[k, i * rows:(i + 1) * rows, :]
        left, right = plane_ref[0], plane_ref[1]
        pq_ref[:, 0, :] = left
        pq_ref[:, 1, :] = right
        planes = [planes[0] + left] + planes[1:-1] + [planes[-1] + right]
        return y_natural(solve(planes, pivots_y)), pq_ref[:, 0:1, :], pq_ref[:, 1:2, :]

    for copy in loads[3:]:
        copy.wait()
    interim_y = h_ref[1] - half_step * forward_z(e_ref[0])
    for copy, _, receives in halos:
        pl.when(receives)(copy.wait_recv)
    interim_z = h_ref[2] - half_step * forward_x(e_ref[1], halo_xr[0:1])
    rows_center_x = y_send_block(
        carry * e_ref[0] + scale * (backward_y(interim_z, 0.0) - backward_z(h_ref[1])),
        interim_z, 1.0, 1,
    )
    pq_ref[:, 0, :] = halo_yr[0]
    pq_ref[:, 1, :] = halo_yr[1]
    ez_above, hx_below = pq_ref[:, 0:1, :], pq_ref[:, 1:2, :]
    rows_center_z = x_send_block(
        carry * e_ref[2] + scale * (backward_x(interim_y, no_x) - backward_y(h_ref[0], hx_below)),
        interim_y, 1.0, 1,
    )
    @pl.when(solving)
    def _():
        y_part(ym_r, ny - 1, 0).wait_recv()
        terms = sweep_matrix(
            *[[ym_r[k, i * rows:(i + 1) * rows, :] for k in range(ny)] for i in range(3)]
        )
        for i, planes in enumerate(terms):
            for k, plane in enumerate(planes):
                sweep_ref[i, k] = plane

    x_all(xm_r, 0).wait_recv()
    first_x = [xm_r[k, 0] for k in range(nx)]
    cross_x = [xm_r[k, 1] for k in range(nx)]
    matrix_x = (first_x, cross_x, sweep_matrix(first_x, cross_x, [xm_r[k, 2] for k in range(nx)]))

    interim_x = h_ref[0] - half_step * forward_y(e_ref[2], ez_above)
    center_y = z_solve(
        carry * e_ref[1] + scale * (backward_z(interim_x) - backward_x(h_ref[2], halo_xr[1:2]))
    )
    curl_x = half_step * forward_z(center_y)
    middle_x = interim_x + curl_x
    second_x = middle_x + curl_x

    y_reduce(1)
    center_z, left, right = x_finish(rows_center_z, 1, matrix_x)
    curl_y = half_step * forward_x(center_z, right)
    middle_y = interim_y + curl_y
    second_y = middle_y + curl_y
    middle_y_below = jnp.where(ix > 0, half_step * (center_z[0:1] - left), 0.0)
    rows_final_z = y_send_block(
        carry * center_z + scale * (backward_x(middle_y, middle_y_below) - backward_y(second_x, 0.0)),
        second_x, -1.0, 2,
    )
    center_x, left, right = y_finish(rows_center_x, 1)
    curl_z = half_step * forward_y(center_x, right)
    middle_z = interim_z + curl_z
    second_z = middle_z + curl_z
    rows_final_y = x_send_block(
        carry * center_y + scale * (backward_z(middle_x) - backward_x(second_z, no_x)),
        second_z, -1.0, 2,
    )
    middle_z_below = jnp.where(iy > 0, half_step * (center_x[:, 0:1, :] - left), 0.0)
    y_reduce(2)
    final_x = z_solve(
        carry * center_x + scale * (backward_y(middle_z, middle_z_below) - backward_z(second_y))
    )
    emit(0, final_x)
    emit(4, second_y - half_step * forward_z(final_x))
    final_y, _, right = x_finish(rows_final_y, 2, matrix_x)
    emit(1, final_y)
    emit(5, second_z - half_step * forward_x(final_y, right))
    final_z, _, right = y_finish(rows_final_z, 2)
    emit(2, final_z)
    emit(3, second_x - half_step * forward_y(final_z, right))

    for k in range(6):
        pltpu.make_async_copy(out_ref.at[k], out[k], store.at[k]).wait()
    for copy, sends, _ in halos:
        pl.when(sends)(copy.wait_send)
    for phase, buffer in enumerate([xm_r, xa_r.at[0], xa_r.at[1]]):
        x_all(buffer, phase).wait_send()
    for phase, buffer in enumerate([ym_s, ya_s.at[0], ya_s.at[1]]):
        y_from_solvers(buffer, phase, True)

    @pl.when(solving)
    def _():
        for phase in (3, 4):
            y_part(yb_s.at[phase - 3], ny - 1, phase).wait_send()


def write_out(e_ref, h_ref, e_out, h_out, done):
    copies = [
        pltpu.make_async_copy(src.at[k], dst.at[k], done.at[i, k])
        for i, (src, dst) in enumerate([(e_ref, e_out), (h_ref, h_out)])
        for k in range(3)
    ]
    for copy in copies:
        copy.start()
    for copy in copies:
        copy.wait()


def per_device(nx, ny, electric, magnetic, material, permittivity, conductivity):
    cx, cy, cz = material.shape
    ns, _ = solvers(ny)
    rows = cx // ns
    cell = (cx, cy, cz)
    vmem, smem = pltpu.VMEM, pltpu.SMEM
    in_hbm = pl.BlockSpec(memory_space=pltpu.HBM)

    def f32(*shape):
        return vmem(shape, jnp.float32)

    dma = pltpu.SemaphoreType.DMA
    fields = (jax.ShapeDtypeStruct((3,) + cell, jnp.float32),) * 2
    advanced = pl.pallas_call(
        functools.partial(kernel, nx, ny),
        out_shape=fields,
        in_specs=[in_hbm] * 5,
        out_specs=(in_hbm,) * 2,
        scratch_shapes=[
            f32(3, *cell), f32(3, *cell), vmem(cell, jnp.int32),
            smem(permittivity.shape, jnp.float32), smem(conductivity.shape, jnp.float32),
            f32(2, cy, cz), f32(2, cx, cz),
            f32(3, cy, cz), f32(nx, 3, cy, cz), f32(2, 2, cy, cz), f32(2, nx, 2, cy, cz),
            f32(ns, 3 * rows, cz), f32(ny, 3 * rows, cz),
            f32(2, ns, 2 * rows, cz), f32(2, ny, 2 * rows, cz),
            f32(2, ny, 2 * rows, cz), f32(2, ns, 2 * rows, cz), f32(3, ny + 1, rows, cz),
            f32(nx + 1, cy, cz), f32(nx + 1, cy, cz), f32(*cell), f32(3, cx, cz),
            f32(cz // 128, cx * cy, 128), f32(cz, cx * cy), f32(6, *cell),
            dma((5,)), dma((6,)), dma((4,)), dma((4,)), dma((3,)), dma((3,)), dma((5,)), dma((5,)),
        ],
        compiler_params=pltpu.CompilerParams(
            collective_id=0, has_side_effects=True, vmem_limit_bytes=62 * 1024 * 1024
        ),
    )(electric, magnetic, material, permittivity, conductivity)
    return pl.pallas_call(
        write_out,
        out_shape=fields,
        in_specs=[in_hbm] * 2,
        out_specs=(in_hbm,) * 2,
        scratch_shapes=[dma((2, 3))],
        compiler_params=pltpu.CompilerParams(vmem_limit_bytes=62 * 1024 * 1024),
    )(*advanced)


def solution(mesh):
    nx, ny = mesh.shape["gx"], mesh.shape["gy"]
    return jax.shard_map(
        functools.partial(per_device, nx, ny),
        mesh=mesh,
        in_specs=(
            P(None, "gx", "gy", None),
            P(None, "gx", "gy", None),
            P("gx", "gy", None),
            P(),
            P(),
        ),
        out_specs=(P(None, "gx", "gy", None), P(None, "gx", "gy", None)),
        check_vma=False,
    )
```

```python
import functools

import jax
import jax.numpy as jnp
from jax import lax
from jax.experimental import pallas as pl
from jax.experimental.pallas import tpu as pltpu
from jax.sharding import PartitionSpec as P

half_step = 12.0
MESH = pl.DeviceIdType.MESH


def strides(length):
    found, stride = [], 1
    while stride < length:
        found.append(stride)
        stride *= 2
    return found


def roll(v, by, axis):
    return pltpu.roll(v, by % v.shape[axis], axis)


def position(shape, axis):
    return lax.broadcasted_iota(jnp.int32, shape, axis)


def reduce_matrix(diagonal, above):
    length, levels = diagonal.shape[0], []
    for stride in strides(length):
        inverse = 1.0 / diagonal
        below = roll(above, stride, 0)
        from_below = -below * roll(inverse, stride, 0)
        from_above = -above * roll(inverse, -stride, 0)
        levels.append((stride, from_below, from_above))
        diagonal = diagonal + from_below * below + from_above * above
        if 2 * stride < length:
            above = from_above * roll(above, -stride, 0)
    return levels, 1.0 / diagonal


def reduce_source(source, system):
    levels, inverse = system
    for stride, from_below, from_above in levels:
        source = source + from_below * roll(source, stride, 0) + from_above * roll(source, -stride, 0)
    return source * inverse


def eliminate(systems):
    found = [[1.0 / diagonals[0]] for diagonals in systems]
    for k in range(1, max(len(diagonals) for diagonals in systems)):
        for diagonals, pivots in zip(systems, found):
            if k < len(diagonals):
                pivots.append(1.0 / (diagonals[k] - pivots[-1]))
    return found


def back(rows, pivots):
    result = [rows[-1]]
    for row, pivot in zip(rows[-2::-1], pivots[-2::-1]):
        result.append(row + pivot * result[-1])
    return result[::-1]


def solve(rows, pivots):
    done = [rows[0] * pivots[0]]
    for row, pivot in zip(rows[1:], pivots[1:]):
        done.append((row + done[-1]) * pivot)
    return back(done, pivots)


def corners(pivots):
    done = [pivots[0]]
    for pivot in pivots[1:]:
        done.append(done[-1] * pivot)
    last = [pivots[-1]]
    for pivot in pivots[-2::-1]:
        last.append(last[-1] * pivot)
    return back(done, pivots), last[::-1]


def dot(left, right):
    terms = [a * b for a, b in zip(left, right)]
    while len(terms) > 1:
        terms = [sum(terms[i:i + 2][1:], terms[i]) for i in range(0, len(terms), 2)]
    return terms[0]


def sweep_matrix(first, cross, last):
    gain, pivots, mults, gains = jnp.zeros_like(first[0]), [], [], []
    for k in range(len(first)):
        pivot = 1.0 / (1.0 - first[k] * gain)
        mult = cross[k] * pivot
        pivots.append(pivot)
        mults.append(mult)
        gains.append(gain)
        gain = last[k] + mult * gain * cross[k]
    gains.append(gain)
    return pivots, mults, gains


def sweep(first, cross, matrix, w_first, w_last):
    pivots, mults, gains = matrix
    count = len(first)
    sums = [jnp.zeros_like(w_first[0])]
    for k in range(count):
        sums.append(w_last[k] + mults[k] * (sums[k] + gains[k] * w_first[k]))
    p, q = [None] * count, [None] * (count + 1)
    q[count] = jnp.zeros_like(w_first[0])
    for k in reversed(range(count)):
        p[k] = sums[k + 1] + gains[k + 1] * q[k + 1]
        q[k] = pivots[k] * (w_first[k] + first[k] * sums[k] + cross[k] * q[k + 1])
    return p, q


def solvers(ny):
    return (ny // 2, ny // 4) if ny % 4 == 0 else (ny, 0)


def kernel(
    nx, ny,
    e_in, h_in, mat_in, eps_in, sig_in, out,
    e_ref, h_ref, mat_ref, eps_ref, sig_ref,
    halo_xr, halo_yr,
    xm_s, xm_r, xa_s, xa_r, ym_s, ym_r, ya_s, ya_r, yb_s, yb_r, sweep_ref,
    p_ref, q_ref, pq_ref, plane_ref, yt_ref, zt_ref, out_ref,
    load, store, halo_send, halo_recv, x_send, x_recv, y_send, y_recv,
):
    cx, cy, cz = mat_ref.shape
    ns, s0 = solvers(ny)
    rows = cx // ns
    lanes = yt_ref.shape[2]
    ix, iy = lax.axis_index("gx"), lax.axis_index("gy")
    solving = (iy >= s0) & (iy < s0 + ns)
    x_others = [lax.rem(ix + d, nx) for d in range(1, nx)]
    y_others = [lax.rem(iy + d, ny) for d in range(1, ny)]

    loads = [
        pltpu.make_async_copy(src, dst, load.at[k])
        for k, (src, dst) in enumerate(
            [(mat_in, mat_ref), (eps_in, eps_ref), (sig_in, sig_ref), (e_in, e_ref), (h_in, h_ref)]
        )
    ]
    for copy in loads:
        copy.start()
    halo_xr[...] = jnp.zeros_like(halo_xr)
    halo_yr[...] = jnp.zeros_like(halo_yr)
    barrier = pltpu.get_barrier_semaphore()
    for other in x_others:
        pl.semaphore_signal(barrier, inc=1, device_id=(other, iy), device_id_type=MESH)
    for other in y_others:
        pl.semaphore_signal(barrier, inc=1, device_id=(ix, other), device_id_type=MESH)
    pl.semaphore_wait(barrier, nx + ny - 2)

    def halo(src, dst, k, to):
        return pltpu.make_async_remote_copy(
            src_ref=src, dst_ref=dst, send_sem=halo_send.at[k], recv_sem=halo_recv.at[k],
            device_id=to, device_id_type=MESH,
        )

    halos = [
        (halo(e_in.at[1, 0], halo_xr.at[0], 0, (lax.rem(ix + nx - 1, nx), iy)), ix > 0, ix < nx - 1),
        (halo(h_in.at[2, cx - 1], halo_xr.at[1], 1, (lax.rem(ix + 1, nx), iy)), ix < nx - 1, ix > 0),
        (halo(e_in.at[2, :, 0], halo_yr.at[0], 2, (ix, lax.rem(iy + ny - 1, ny))), iy > 0, iy < ny - 1),
        (halo(h_in.at[0, :, cy - 1], halo_yr.at[1], 3, (ix, lax.rem(iy + 1, ny))), iy < ny - 1, iy > 0),
    ]
    for copy, sends, _ in halos:
        pl.when(sends)(copy.start)
    for copy in loads[:3]:
        copy.wait()

    material = mat_ref[...]
    excess = jnp.zeros(material.shape, jnp.float32)
    carry = jnp.zeros(material.shape, jnp.float32)
    for row in range(eps_ref.shape[0]):
        permit = eps_ref[row] * (1.0 / half_step)
        lossy = sig_ref[row] * 0.5
        chosen = material == row
        excess = jnp.where(chosen, (permit + lossy) * (1.0 / half_step), excess)
        carry = jnp.where(chosen, (permit - lossy) * (1.0 / half_step), carry)

    def emit(k, value):
        out_ref[k] = value
        pltpu.make_async_copy(out_ref.at[k], out.at[k], store.at[k]).start()

    def x_copy(src, dst, phase, to):
        return pltpu.make_async_remote_copy(
            src_ref=src, dst_ref=dst, send_sem=x_send.at[phase], recv_sem=x_recv.at[phase],
            device_id=(to, iy), device_id_type=MESH,
        )

    def x_start(src, buffer, phase):
        for other in x_others:
            x_copy(src, buffer.at[ix], phase, other).start()
        buffer[ix] = src[...]

    def x_all(buffer, phase):
        part = buffer.at[pl.ds(0, nx - 1)]
        return x_copy(part, part, phase, x_others[0])

    def y_copy(src, dst, phase, to):
        return pltpu.make_async_remote_copy(
            src_ref=src, dst_ref=dst, send_sem=y_send.at[phase], recv_sem=y_recv.at[phase],
            device_id=(ix, to), device_id_type=MESH,
        )

    def y_gather(src, buffer, phase):
        for d in range(ns):
            s = lax.rem(iy + d, ns)
            copy = y_copy(src.at[s], buffer.at[iy], phase, s0 + s)
            pl.when(iy != s0 + s)(copy.start)

        @pl.when(solving)
        def _():
            buffer[iy] = src[iy - s0]

    def y_scatter(src, buffer, phase):
        for other in y_others:
            y_copy(src.at[other], buffer.at[iy - s0], phase, other).start()
        buffer[iy - s0] = src[iy]

    def y_part(buffer, count, phase):
        part = buffer.at[pl.ds(0, count)]
        return y_copy(part, part, phase, y_others[0])

    def y_from_solvers(buffer, phase, send):
        for when, count in ((solving, ns - 1), (jnp.logical_not(solving), ns)):
            if count:
                copy = y_part(buffer, count, phase)
                pl.when(when)(copy.wait_send if send else copy.wait_recv)

    def y_pack(buffer, planes):
        for i, plane in enumerate(planes):
            plane_ref[i] = plane
        for k in range(ns):
            for i in range(len(planes)):
                buffer[k, i * rows:(i + 1) * rows, :] = plane_ref[i, k * rows:(k + 1) * rows, :]

    def y_store(v):
        flat = v.reshape(cx * cy, cz)
        for half in range(cz // lanes):
            yt_ref[half] = flat[:, half * lanes:(half + 1) * lanes]

    def y_row(k):
        return jnp.concatenate(
            [yt_ref[half, pl.ds(k, cx, stride=cy), :] for half in range(cz // lanes)], axis=1
        )

    def y_rows(v):
        y_store(v)
        return [y_row(k) for k in range(cy)]

    def y_natural(planes):
        for k, plane in enumerate(planes):
            for half in range(cz // lanes):
                yt_ref[half, pl.ds(k, cx, stride=cy), :] = plane[:, half * lanes:(half + 1) * lanes]
        return jnp.concatenate(
            [yt_ref[half] for half in range(cz // lanes)], axis=1
        ).reshape(cx, cy, cz)

    at_y, at_z = position(material.shape, 1), position(material.shape, 2)
    diagonal = excess + 2.0

    block = zt_ref.shape[0] // 16
    count = cz // block

    def z_rows(v):
        zt_ref[...] = v.reshape(cx * cy, cz).T
        return [zt_ref[pl.ds(k, count, stride=block), :] for k in range(block)]

    lines_x = [diagonal[k] for k in range(cx)]
    lines_x[0] = jnp.where(ix == 0, lines_x[0] - 1.0, lines_x[0])
    lines_y = y_rows(diagonal)
    lines_y[0] = jnp.where(iy == 0, lines_y[0] - 1.0, lines_y[0])
    pivots_x, pivots_y = eliminate([lines_x, lines_y])
    left_y, right_y = corners(pivots_y)
    left_x, right_x = corners(pivots_x)
    y_pack(ym_s, [left_y[0], right_y[0], right_y[-1]])
    y_gather(ym_s, ym_r, 0)
    xm_s[0] = left_x[0]
    xm_s[1] = right_x[0]
    xm_s[2] = right_x[-1]
    x_start(xm_s, xm_r, 0)
    def z_solve(v):
        planes = z_rows(v)
        inner, edge = planes[:-1], planes[-1]
        edge = edge + dot(right_z, inner) + jnp.where(
            at_block == count - 1, 0.0, roll(dot(left_z, inner), -1, 0)
        )
        edge = reduce_source(edge, system_z)
        inner[0] = inner[0] + jnp.where(at_block == 0, 0.0, roll(edge, 1, 0))
        inner[-1] = inner[-1] + edge
        for k, plane in enumerate(solve(inner, pivots_z) + [edge]):
            zt_ref[pl.ds(k, count, stride=block), :] = plane
        return zt_ref[...].T.reshape(cx, cy, cz)

    def forward_z(v):
        return jnp.where(at_z == cz - 1, 0.0, roll(v, -1, 2)) - v

    def backward_z(v):
        return v - jnp.where(at_z == 0, 0.0, roll(v, 1, 2))

    def forward_y(v, upper):
        return jnp.where(at_y == cy - 1, upper, roll(v, -1, 1)) - v

    def backward_y(v, lower):
        return v - jnp.where(at_y == 0, lower, roll(v, 1, 1))

    def forward_x(v, upper):
        return jnp.concatenate([v[1:], upper], axis=0) - v

    def backward_x(v, lower):
        return v - jnp.concatenate([lower, v[:-1]], axis=0)

    no_x = jnp.zeros((1, cy, cz), jnp.float32)
    scale = 1.0 / half_step

    def x_send_block(source, absorbed, sign, phase):
        planes = [source[k] for k in range(cx)]
        xa_s[phase - 1, 0] = dot(left_x, planes)
        xa_s[phase - 1, 1] = dot(right_x, planes) - (sign * scale) * absorbed[cx - 1]
        x_start(xa_s.at[phase - 1], xa_r.at[phase - 1], phase)
        return planes

    def y_send_block(source, absorbed, sign, phase):
        y_store(absorbed)
        last = y_row(cy - 1)
        planes = y_rows(source)
        y_pack(
            ya_s.at[phase - 1], [dot(left_y, planes), dot(right_y, planes) - (sign * scale) * last]
        )
        y_gather(ya_s.at[phase - 1], ya_r.at[phase - 1], phase)
        return planes

    def x_finish(planes, phase, matrix):
        first, cross, terms = matrix
        x_all(xa_r.at[phase - 1], phase).wait_recv()
        p, q = sweep(
            first, cross, terms,
            [xa_r[phase - 1, k, 0] for k in range(nx)], [xa_r[phase - 1, k, 1] for k in range(nx)],
        )
        p_ref[0] = jnp.zeros_like(p[0])
        for k in range(nx):
            p_ref[k + 1] = p[k]
            q_ref[k] = q[k]
        q_ref[nx] = q[nx]
        left, right = p_ref[ix], q_ref[ix + 1]
        planes = [planes[0] + left] + planes[1:-1] + [planes[-1] + right]
        return jnp.stack(solve(planes, pivots_x)), left[None], right[None]

    def y_reduce(phase):
        @pl.when(solving)
        def _():
            buffer = ya_r.at[phase - 1]
            y_part(buffer, ny - 1, phase).wait_recv()
            p, q = sweep(
                [ym_r[k, 0:rows, :] for k in range(ny)],
                [ym_r[k, rows:2 * rows, :] for k in range(ny)],
                [[sweep_ref[i, k] for k in range(ny + 1 if i == 2 else ny)] for i in range(3)],
                [buffer[k, 0:rows, :] for k in range(ny)],
                [buffer[k, rows:2 * rows, :] for k in range(ny)],
            )
            out = yb_s.at[phase - 1]
            for k in range(ny):
                out[k, 0:rows, :] = p[k - 1] if k else jnp.zeros_like(p[0])
                out[k, rows:2 * rows, :] = q[k + 1]
            y_scatter(out, yb_r.at[phase - 1], phase + 2)

    def y_finish(planes, phase):
        buffer = yb_r.at[phase - 1]
        y_from_solvers(buffer, phase + 2, False)
        for k in range(ns):
            for i in range(2):
                plane_ref[i, k * rows:(k + 1) * rows, :] = buffer[k, i * rows:(i + 1) * rows, :]
        left, right = plane_ref[0], plane_ref[1]
        pq_ref[:, 0, :] = left
        pq_ref[:, 1, :] = right
        planes = [planes[0] + left] + planes[1:-1] + [planes[-1] + right]
        return y_natural(solve(planes, pivots_y)), pq_ref[:, 0:1, :], pq_ref[:, 1:2, :]

    for copy in loads[3:]:
        copy.wait()
    interim_y = h_ref[1] - half_step * forward_z(e_ref[0])
    for copy, _, receives in halos:
        pl.when(receives)(copy.wait_recv)
    interim_z = h_ref[2] - half_step * forward_x(e_ref[1], halo_xr[0:1])
    rows_center_x = y_send_block(
        carry * e_ref[0] + scale * (backward_y(interim_z, 0.0) - backward_z(h_ref[1])),
        interim_z, 1.0, 1,
    )
    pq_ref[:, 0, :] = halo_yr[0]
    pq_ref[:, 1, :] = halo_yr[1]
    ez_above, hx_below = pq_ref[:, 0:1, :], pq_ref[:, 1:2, :]
    rows_center_z = x_send_block(
        carry * e_ref[2] + scale * (backward_x(interim_y, no_x) - backward_y(h_ref[0], hx_below)),
        interim_y, 1.0, 1,
    )
    lines_z = z_rows(jnp.where(at_z == 0, diagonal - 1.0, diagonal))
    (pivots_z,) = eliminate([lines_z[:-1]])
    left_z, right_z = corners(pivots_z)
    at_block = position(lines_z[0].shape, 0)
    inside = at_block < count - 1
    system_z = reduce_matrix(
        lines_z[-1] - right_z[-1] - jnp.where(inside, roll(left_z[0], -1, 0), 0.0),
        jnp.where(inside, -roll(right_z[0], -1, 0), 0.0),
    )

    @pl.when(solving)
    def _():
        y_part(ym_r, ny - 1, 0).wait_recv()
        terms = sweep_matrix(
            *[[ym_r[k, i * rows:(i + 1) * rows, :] for k in range(ny)] for i in range(3)]
        )
        for i, planes in enumerate(terms):
            for k, plane in enumerate(planes):
                sweep_ref[i, k] = plane

    y_reduce(1)
    x_all(xm_r, 0).wait_recv()
    first_x = [xm_r[k, 0] for k in range(nx)]
    cross_x = [xm_r[k, 1] for k in range(nx)]
    matrix_x = (first_x, cross_x, sweep_matrix(first_x, cross_x, [xm_r[k, 2] for k in range(nx)]))

    interim_x = h_ref[0] - half_step * forward_y(e_ref[2], ez_above)
    center_y = z_solve(
        carry * e_ref[1] + scale * (backward_z(interim_x) - backward_x(h_ref[2], halo_xr[1:2]))
    )
    curl_x = half_step * forward_z(center_y)
    middle_x = interim_x + curl_x
    second_x = middle_x + curl_x

    center_z, left, right = x_finish(rows_center_z, 1, matrix_x)
    curl_y = half_step * forward_x(center_z, right)
    middle_y = interim_y + curl_y
    second_y = middle_y + curl_y
    middle_y_below = jnp.where(ix > 0, half_step * (center_z[0:1] - left), 0.0)
    rows_final_z = y_send_block(
        carry * center_z + scale * (backward_x(middle_y, middle_y_below) - backward_y(second_x, 0.0)),
        second_x, -1.0, 2,
    )
    center_x, left, right = y_finish(rows_center_x, 1)
    curl_z = half_step * forward_y(center_x, right)
    middle_z = interim_z + curl_z
    second_z = middle_z + curl_z
    rows_final_y = x_send_block(
        carry * center_y + scale * (backward_z(middle_x) - backward_x(second_z, no_x)),
        second_z, -1.0, 2,
    )
    middle_z_below = jnp.where(iy > 0, half_step * (center_x[:, 0:1, :] - left), 0.0)
    y_reduce(2)
    final_x = z_solve(
        carry * center_x + scale * (backward_y(middle_z, middle_z_below) - backward_z(second_y))
    )
    emit(0, final_x)
    emit(4, second_y - half_step * forward_z(final_x))
    final_y, _, right = x_finish(rows_final_y, 2, matrix_x)
    emit(1, final_y)
    emit(5, second_z - half_step * forward_x(final_y, right))
    final_z, _, right = y_finish(rows_final_z, 2)
    emit(2, final_z)
    emit(3, second_x - half_step * forward_y(final_z, right))

    for k in range(6):
        pltpu.make_async_copy(out_ref.at[k], out.at[k], store.at[k]).wait()
    for copy, sends, _ in halos:
        pl.when(sends)(copy.wait_send)
    for phase, buffer in enumerate([xm_r, xa_r.at[0], xa_r.at[1]]):
        x_all(buffer, phase).wait_send()
    for phase, buffer in enumerate([ym_s, ya_s.at[0], ya_s.at[1]]):
        y_from_solvers(buffer, phase, True)

    @pl.when(solving)
    def _():
        for phase in (3, 4):
            y_part(yb_s.at[phase - 3], ny - 1, phase).wait_send()


def per_device(nx, ny, electric, magnetic, material, permittivity, conductivity):
    cx, cy, cz = material.shape
    ns, _ = solvers(ny)
    rows = cx // ns
    cell = (cx, cy, cz)
    vmem, smem = pltpu.VMEM, pltpu.SMEM
    in_hbm = pl.BlockSpec(memory_space=pltpu.HBM)

    def f32(*shape):
        return vmem(shape, jnp.float32)

    dma = pltpu.SemaphoreType.DMA
    advanced = pl.pallas_call(
        functools.partial(kernel, nx, ny),
        out_shape=jax.ShapeDtypeStruct((6,) + cell, jnp.float32),
        in_specs=[in_hbm] * 5,
        out_specs=in_hbm,
        scratch_shapes=[
            f32(3, *cell), f32(3, *cell), vmem(cell, jnp.int32),
            smem(permittivity.shape, jnp.float32), smem(conductivity.shape, jnp.float32),
            f32(2, cy, cz), f32(2, cx, cz),
            f32(3, cy, cz), f32(nx, 3, cy, cz), f32(2, 2, cy, cz), f32(2, nx, 2, cy, cz),
            f32(ns, 3 * rows, cz), f32(ny, 3 * rows, cz),
            f32(2, ns, 2 * rows, cz), f32(2, ny, 2 * rows, cz),
            f32(2, ny, 2 * rows, cz), f32(2, ns, 2 * rows, cz), f32(3, ny + 1, rows, cz),
            f32(nx + 1, cy, cz), f32(nx + 1, cy, cz), f32(*cell), f32(3, cx, cz),
            f32(cz // 128, cx * cy, 128), f32(cz, cx * cy), f32(6, *cell),
            dma((5,)), dma((6,)), dma((4,)), dma((4,)), dma((3,)), dma((3,)), dma((5,)), dma((5,)),
        ],
        compiler_params=pltpu.CompilerParams(
            collective_id=0, has_side_effects=True, vmem_limit_bytes=62 * 1024 * 1024
        ),
    )(electric, magnetic, material, permittivity, conductivity)
    return advanced[:3], advanced[3:]


def solution(mesh):
    nx, ny = mesh.shape["gx"], mesh.shape["gy"]
    return jax.shard_map(
        functools.partial(per_device, nx, ny),
        mesh=mesh,
        in_specs=(
            P(None, "gx", "gy", None),
            P(None, "gx", "gy", None),
            P("gx", "gy", None),
            P(),
            P(),
        ),
        out_specs=(P(None, "gx", "gy", None), P(None, "gx", "gy", None)),
        check_vma=False,
    )
```

```python
import functools

import jax
import jax.numpy as jnp
from jax import lax
from jax.experimental import pallas as pl
from jax.experimental.pallas import tpu as pltpu
from jax.sharding import PartitionSpec as P

half_step = 12.0
MESH = pl.DeviceIdType.MESH


def strides(length):
    found, stride = [], 1
    while stride < length:
        found.append(stride)
        stride *= 2
    return found


def roll(v, by, axis):
    return pltpu.roll(v, by % v.shape[axis], axis)


def position(shape, axis):
    return lax.broadcasted_iota(jnp.int32, shape, axis)


def inverse_of(v):
    guess = pl.reciprocal(v, approx=True)
    guess = guess * (2.0 - v * guess)
    return guess * (2.0 - v * guess)


def reduce_matrix(diagonal, above):
    length, levels = diagonal.shape[0], []
    for stride in strides(length):
        inverse = inverse_of(diagonal)
        below = roll(above, stride, 0)
        from_below = -below * roll(inverse, stride, 0)
        from_above = -above * roll(inverse, -stride, 0)
        levels.append((stride, from_below, from_above))
        diagonal = diagonal + from_below * below + from_above * above
        if 2 * stride < length:
            above = from_above * roll(above, -stride, 0)
    return levels, inverse_of(diagonal)


def reduce_source(source, system):
    levels, inverse = system
    for stride, from_below, from_above in levels:
        source = source + from_below * roll(source, stride, 0) + from_above * roll(source, -stride, 0)
    return source * inverse


def eliminate(systems):
    found = [[inverse_of(diagonals[0])] for diagonals in systems]
    for k in range(1, max(len(diagonals) for diagonals in systems)):
        for diagonals, pivots in zip(systems, found):
            if k < len(diagonals):
                pivots.append(inverse_of(diagonals[k] - pivots[-1]))
    return found


def back(rows, pivots):
    result = [rows[-1]]
    for row, pivot in zip(rows[-2::-1], pivots[-2::-1]):
        result.append(row + pivot * result[-1])
    return result[::-1]


def solve(rows, pivots):
    done = [rows[0] * pivots[0]]
    for row, pivot in zip(rows[1:], pivots[1:]):
        done.append((row + done[-1]) * pivot)
    return back(done, pivots)


def corners(pivots):
    done = [pivots[0]]
    for pivot in pivots[1:]:
        done.append(done[-1] * pivot)
    last = [pivots[-1]]
    for pivot in pivots[-2::-1]:
        last.append(last[-1] * pivot)
    return back(done, pivots), last[::-1]


def dot(left, right):
    terms = [a * b for a, b in zip(left, right)]
    while len(terms) > 1:
        terms = [sum(terms[i:i + 2][1:], terms[i]) for i in range(0, len(terms), 2)]
    return terms[0]


def sweep_matrix(first, cross, last):
    gain, pivots, mults, gains = jnp.zeros_like(first[0]), [], [], []
    for k in range(len(first)):
        pivot = inverse_of(1.0 - first[k] * gain)
        mult = cross[k] * pivot
        pivots.append(pivot)
        mults.append(mult)
        gains.append(gain)
        gain = last[k] + mult * gain * cross[k]
    gains.append(gain)
    return pivots, mults, gains


def sweep(first, cross, matrix, w_first, w_last):
    pivots, mults, gains = matrix
    count = len(first)
    sums = [jnp.zeros_like(w_first[0])]
    for k in range(count):
        sums.append(w_last[k] + mults[k] * (sums[k] + gains[k] * w_first[k]))
    p, q = [None] * count, [None] * (count + 1)
    q[count] = jnp.zeros_like(w_first[0])
    for k in reversed(range(count)):
        p[k] = sums[k + 1] + gains[k + 1] * q[k + 1]
        q[k] = pivots[k] * (w_first[k] + first[k] * sums[k] + cross[k] * q[k + 1])
    return p, q


def solvers(ny):
    return (ny // 2, ny // 4) if ny % 4 == 0 else (ny, 0)


def kernel(
    nx, ny,
    e_in, h_in, mat_in, eps_in, sig_in, out,
    e_ref, h_ref, mat_ref, eps_ref, sig_ref,
    halo_xr, halo_yr,
    xm_s, xm_r, xa_s, xa_r, ym_s, ym_r, ya_s, ya_r, yb_s, yb_r, sweep_ref,
    p_ref, q_ref, pq_ref, plane_ref, yt_ref, zt_ref, out_ref,
    load, store, halo_send, halo_recv, x_send, x_recv, y_send, y_recv,
):
    cx, cy, cz = mat_ref.shape
    ns, s0 = solvers(ny)
    rows = cx // ns
    lanes = yt_ref.shape[2]
    ix, iy = lax.axis_index("gx"), lax.axis_index("gy")
    solving = (iy >= s0) & (iy < s0 + ns)
    x_others = [lax.rem(ix + d, nx) for d in range(1, nx)]
    y_others = [lax.rem(iy + d, ny) for d in range(1, ny)]

    loads = [
        pltpu.make_async_copy(src, dst, load.at[k])
        for k, (src, dst) in enumerate(
            [(mat_in, mat_ref), (eps_in, eps_ref), (sig_in, sig_ref), (e_in, e_ref), (h_in, h_ref)]
        )
    ]
    for copy in loads:
        copy.start()
    halo_xr[...] = jnp.zeros_like(halo_xr)
    halo_yr[...] = jnp.zeros_like(halo_yr)
    barrier = pltpu.get_barrier_semaphore()
    for other in x_others:
        pl.semaphore_signal(barrier, inc=1, device_id=(other, iy), device_id_type=MESH)
    for other in y_others:
        pl.semaphore_signal(barrier, inc=1, device_id=(ix, other), device_id_type=MESH)
    pl.semaphore_wait(barrier, nx + ny - 2)

    def halo(src, dst, k, to):
        return pltpu.make_async_remote_copy(
            src_ref=src, dst_ref=dst, send_sem=halo_send.at[k], recv_sem=halo_recv.at[k],
            device_id=to, device_id_type=MESH,
        )

    halos = [
        (halo(e_in.at[1, 0], halo_xr.at[0], 0, (lax.rem(ix + nx - 1, nx), iy)), ix > 0, ix < nx - 1),
        (halo(h_in.at[2, cx - 1], halo_xr.at[1], 1, (lax.rem(ix + 1, nx), iy)), ix < nx - 1, ix > 0),
        (halo(e_in.at[2, :, 0], halo_yr.at[0], 2, (ix, lax.rem(iy + ny - 1, ny))), iy > 0, iy < ny - 1),
        (halo(h_in.at[0, :, cy - 1], halo_yr.at[1], 3, (ix, lax.rem(iy + 1, ny))), iy < ny - 1, iy > 0),
    ]
    for copy, sends, _ in halos:
        pl.when(sends)(copy.start)
    for copy in loads[:3]:
        copy.wait()

    material = mat_ref[...]
    excess = jnp.zeros(material.shape, jnp.float32)
    carry = jnp.zeros(material.shape, jnp.float32)
    for row in range(eps_ref.shape[0]):
        permit = eps_ref[row] * (1.0 / half_step)
        lossy = sig_ref[row] * 0.5
        chosen = material == row
        excess = jnp.where(chosen, (permit + lossy) * (1.0 / half_step), excess)
        carry = jnp.where(chosen, (permit - lossy) * (1.0 / half_step), carry)

    def emit(k, value):
        out_ref[k] = value
        pltpu.make_async_copy(out_ref.at[k], out.at[k], store.at[k]).start()

    def x_copy(src, dst, phase, to):
        return pltpu.make_async_remote_copy(
            src_ref=src, dst_ref=dst, send_sem=x_send.at[phase], recv_sem=x_recv.at[phase],
            device_id=(to, iy), device_id_type=MESH,
        )

    def x_start(src, buffer, phase):
        for other in x_others:
            x_copy(src, buffer.at[ix], phase, other).start()
        buffer[ix] = src[...]

    def x_all(buffer, phase):
        part = buffer.at[pl.ds(0, nx - 1)]
        return x_copy(part, part, phase, x_others[0])

    def y_copy(src, dst, phase, to):
        return pltpu.make_async_remote_copy(
            src_ref=src, dst_ref=dst, send_sem=y_send.at[phase], recv_sem=y_recv.at[phase],
            device_id=(ix, to), device_id_type=MESH,
        )

    def y_gather(src, buffer, phase):
        for d in range(ns):
            s = lax.rem(iy + d, ns)
            copy = y_copy(src.at[s], buffer.at[iy], phase, s0 + s)
            pl.when(iy != s0 + s)(copy.start)

        @pl.when(solving)
        def _():
            buffer[iy] = src[iy - s0]

    def y_scatter(src, buffer, phase):
        for other in y_others:
            y_copy(src.at[other], buffer.at[iy - s0], phase, other).start()
        buffer[iy - s0] = src[iy]

    def y_part(buffer, count, phase):
        part = buffer.at[pl.ds(0, count)]
        return y_copy(part, part, phase, y_others[0])

    def y_from_solvers(buffer, phase, send):
        for when, count in ((solving, ns - 1), (jnp.logical_not(solving), ns)):
            if count:
                copy = y_part(buffer, count, phase)
                pl.when(when)(copy.wait_send if send else copy.wait_recv)

    def y_pack(buffer, planes):
        for i, plane in enumerate(planes):
            plane_ref[i] = plane
        for k in range(ns):
            for i in range(len(planes)):
                buffer[k, i * rows:(i + 1) * rows, :] = plane_ref[i, k * rows:(k + 1) * rows, :]

    def y_store(v):
        flat = v.reshape(cx * cy, cz)
        for half in range(cz // lanes):
            yt_ref[half] = flat[:, half * lanes:(half + 1) * lanes]

    def y_row(k):
        return jnp.concatenate(
            [yt_ref[half, pl.ds(k, cx, stride=cy), :] for half in range(cz // lanes)], axis=1
        )

    def y_rows(v):
        y_store(v)
        return [y_row(k) for k in range(cy)]

    def y_natural(planes):
        for k, plane in enumerate(planes):
            for half in range(cz // lanes):
                yt_ref[half, pl.ds(k, cx, stride=cy), :] = plane[:, half * lanes:(half + 1) * lanes]
        return jnp.concatenate(
            [yt_ref[half] for half in range(cz // lanes)], axis=1
        ).reshape(cx, cy, cz)

    at_y, at_z = position(material.shape, 1), position(material.shape, 2)
    diagonal = excess + 2.0

    block = zt_ref.shape[0] // 16
    count = cz // block

    def z_rows(v):
        zt_ref[...] = v.reshape(cx * cy, cz).T
        return [zt_ref[pl.ds(k, count, stride=block), :] for k in range(block)]

    lines_x = [diagonal[k] for k in range(cx)]
    lines_x[0] = jnp.where(ix == 0, lines_x[0] - 1.0, lines_x[0])
    lines_y = y_rows(diagonal)
    lines_y[0] = jnp.where(iy == 0, lines_y[0] - 1.0, lines_y[0])
    pivots_x, pivots_y = eliminate([lines_x, lines_y])
    left_y, right_y = corners(pivots_y)
    left_x, right_x = corners(pivots_x)
    y_pack(ym_s, [left_y[0], right_y[0], right_y[-1]])
    y_gather(ym_s, ym_r, 0)
    xm_s[0] = left_x[0]
    xm_s[1] = right_x[0]
    xm_s[2] = right_x[-1]
    x_start(xm_s, xm_r, 0)
    def z_solve(v):
        planes = z_rows(v)
        inner, edge = planes[:-1], planes[-1]
        edge = edge + dot(right_z, inner) + jnp.where(
            at_block == count - 1, 0.0, roll(dot(left_z, inner), -1, 0)
        )
        edge = reduce_source(edge, system_z)
        inner[0] = inner[0] + jnp.where(at_block == 0, 0.0, roll(edge, 1, 0))
        inner[-1] = inner[-1] + edge
        for k, plane in enumerate(solve(inner, pivots_z) + [edge]):
            zt_ref[pl.ds(k, count, stride=block), :] = plane
        return zt_ref[...].T.reshape(cx, cy, cz)

    def forward_z(v):
        return jnp.where(at_z == cz - 1, 0.0, roll(v, -1, 2)) - v

    def backward_z(v):
        return v - jnp.where(at_z == 0, 0.0, roll(v, 1, 2))

    def forward_y(v, upper):
        return jnp.where(at_y == cy - 1, upper, roll(v, -1, 1)) - v

    def backward_y(v, lower):
        return v - jnp.where(at_y == 0, lower, roll(v, 1, 1))

    def forward_x(v, upper):
        return jnp.concatenate([v[1:], upper], axis=0) - v

    def backward_x(v, lower):
        return v - jnp.concatenate([lower, v[:-1]], axis=0)

    no_x = jnp.zeros((1, cy, cz), jnp.float32)
    scale = 1.0 / half_step

    def x_send_block(source, absorbed, sign, phase):
        planes = [source[k] for k in range(cx)]
        xa_s[phase - 1, 0] = dot(left_x, planes)
        xa_s[phase - 1, 1] = dot(right_x, planes) - (sign * scale) * absorbed[cx - 1]
        x_start(xa_s.at[phase - 1], xa_r.at[phase - 1], phase)
        return planes

    def y_send_block(source, absorbed, sign, phase):
        y_store(absorbed)
        last = y_row(cy - 1)
        planes = y_rows(source)
        y_pack(
            ya_s.at[phase - 1], [dot(left_y, planes), dot(right_y, planes) - (sign * scale) * last]
        )
        y_gather(ya_s.at[phase - 1], ya_r.at[phase - 1], phase)
        return planes

    def x_finish(planes, phase, matrix):
        first, cross, terms = matrix
        x_all(xa_r.at[phase - 1], phase).wait_recv()
        p, q = sweep(
            first, cross, terms,
            [xa_r[phase - 1, k, 0] for k in range(nx)], [xa_r[phase - 1, k, 1] for k in range(nx)],
        )
        p_ref[0] = jnp.zeros_like(p[0])
        for k in range(nx):
            p_ref[k + 1] = p[k]
            q_ref[k] = q[k]
        q_ref[nx] = q[nx]
        left, right = p_ref[ix], q_ref[ix + 1]
        planes = [planes[0] + left] + planes[1:-1] + [planes[-1] + right]
        return jnp.stack(solve(planes, pivots_x)), left[None], right[None]

    def y_reduce(phase):
        @pl.when(solving)
        def _():
            buffer = ya_r.at[phase - 1]
            y_part(buffer, ny - 1, phase).wait_recv()
            p, q = sweep(
                [ym_r[k, 0:rows, :] for k in range(ny)],
                [ym_r[k, rows:2 * rows, :] for k in range(ny)],
                [[sweep_ref[i, k] for k in range(ny + 1 if i == 2 else ny)] for i in range(3)],
                [buffer[k, 0:rows, :] for k in range(ny)],
                [buffer[k, rows:2 * rows, :] for k in range(ny)],
            )
            out = yb_s.at[phase - 1]
            for k in range(ny):
                out[k, 0:rows, :] = p[k - 1] if k else jnp.zeros_like(p[0])
                out[k, rows:2 * rows, :] = q[k + 1]
            y_scatter(out, yb_r.at[phase - 1], phase + 2)

    def y_finish(planes, phase):
        buffer = yb_r.at[phase - 1]
        y_from_solvers(buffer, phase + 2, False)
        for k in range(ns):
            for i in range(2):
                plane_ref[i, k * rows:(k + 1) * rows, :] = buffer[k, i * rows:(i + 1) * rows, :]
        left, right = plane_ref[0], plane_ref[1]
        pq_ref[:, 0, :] = left
        pq_ref[:, 1, :] = right
        planes = [planes[0] + left] + planes[1:-1] + [planes[-1] + right]
        return y_natural(solve(planes, pivots_y)), pq_ref[:, 0:1, :], pq_ref[:, 1:2, :]

    for copy in loads[3:]:
        copy.wait()
    interim_y = h_ref[1] - half_step * forward_z(e_ref[0])
    for copy, _, receives in halos:
        pl.when(receives)(copy.wait_recv)
    interim_z = h_ref[2] - half_step * forward_x(e_ref[1], halo_xr[0:1])
    rows_center_x = y_send_block(
        carry * e_ref[0] + scale * (backward_y(interim_z, 0.0) - backward_z(h_ref[1])),
        interim_z, 1.0, 1,
    )
    pq_ref[:, 0, :] = halo_yr[0]
    pq_ref[:, 1, :] = halo_yr[1]
    ez_above, hx_below = pq_ref[:, 0:1, :], pq_ref[:, 1:2, :]
    rows_center_z = x_send_block(
        carry * e_ref[2] + scale * (backward_x(interim_y, no_x) - backward_y(h_ref[0], hx_below)),
        interim_y, 1.0, 1,
    )
    lines_z = z_rows(jnp.where(at_z == 0, diagonal - 1.0, diagonal))
    (pivots_z,) = eliminate([lines_z[:-1]])
    left_z, right_z = corners(pivots_z)
    at_block = position(lines_z[0].shape, 0)
    inside = at_block < count - 1
    system_z = reduce_matrix(
        lines_z[-1] - right_z[-1] - jnp.where(inside, roll(left_z[0], -1, 0), 0.0),
        jnp.where(inside, -roll(right_z[0], -1, 0), 0.0),
    )

    @pl.when(solving)
    def _():
        y_part(ym_r, ny - 1, 0).wait_recv()
        terms = sweep_matrix(
            *[[ym_r[k, i * rows:(i + 1) * rows, :] for k in range(ny)] for i in range(3)]
        )
        for i, planes in enumerate(terms):
            for k, plane in enumerate(planes):
                sweep_ref[i, k] = plane

    y_reduce(1)
    x_all(xm_r, 0).wait_recv()
    first_x = [xm_r[k, 0] for k in range(nx)]
    cross_x = [xm_r[k, 1] for k in range(nx)]
    matrix_x = (first_x, cross_x, sweep_matrix(first_x, cross_x, [xm_r[k, 2] for k in range(nx)]))

    interim_x = h_ref[0] - half_step * forward_y(e_ref[2], ez_above)
    center_y = z_solve(
        carry * e_ref[1] + scale * (backward_z(interim_x) - backward_x(h_ref[2], halo_xr[1:2]))
    )
    curl_x = half_step * forward_z(center_y)
    middle_x = interim_x + curl_x
    second_x = middle_x + curl_x

    center_z, left, right = x_finish(rows_center_z, 1, matrix_x)
    curl_y = half_step * forward_x(center_z, right)
    middle_y = interim_y + curl_y
    second_y = middle_y + curl_y
    middle_y_below = jnp.where(ix > 0, half_step * (center_z[0:1] - left), 0.0)
    rows_final_z = y_send_block(
        carry * center_z + scale * (backward_x(middle_y, middle_y_below) - backward_y(second_x, 0.0)),
        second_x, -1.0, 2,
    )
    center_x, left, right = y_finish(rows_center_x, 1)
    curl_z = half_step * forward_y(center_x, right)
    middle_z = interim_z + curl_z
    second_z = middle_z + curl_z
    rows_final_y = x_send_block(
        carry * center_y + scale * (backward_z(middle_x) - backward_x(second_z, no_x)),
        second_z, -1.0, 2,
    )
    middle_z_below = jnp.where(iy > 0, half_step * (center_x[:, 0:1, :] - left), 0.0)
    y_reduce(2)
    final_x = z_solve(
        carry * center_x + scale * (backward_y(middle_z, middle_z_below) - backward_z(second_y))
    )
    emit(0, final_x)
    emit(4, second_y - half_step * forward_z(final_x))
    final_y, _, right = x_finish(rows_final_y, 2, matrix_x)
    emit(1, final_y)
    emit(5, second_z - half_step * forward_x(final_y, right))
    final_z, _, right = y_finish(rows_final_z, 2)
    emit(2, final_z)
    emit(3, second_x - half_step * forward_y(final_z, right))

    for k in range(6):
        pltpu.make_async_copy(out_ref.at[k], out.at[k], store.at[k]).wait()
    for copy, sends, _ in halos:
        pl.when(sends)(copy.wait_send)
    for phase, buffer in enumerate([xm_r, xa_r.at[0], xa_r.at[1]]):
        x_all(buffer, phase).wait_send()
    for phase, buffer in enumerate([ym_s, ya_s.at[0], ya_s.at[1]]):
        y_from_solvers(buffer, phase, True)

    @pl.when(solving)
    def _():
        for phase in (3, 4):
            y_part(yb_s.at[phase - 3], ny - 1, phase).wait_send()


def per_device(nx, ny, electric, magnetic, material, permittivity, conductivity):
    cx, cy, cz = material.shape
    ns, _ = solvers(ny)
    rows = cx // ns
    cell = (cx, cy, cz)
    vmem, smem = pltpu.VMEM, pltpu.SMEM
    in_hbm = pl.BlockSpec(memory_space=pltpu.HBM)

    def f32(*shape):
        return vmem(shape, jnp.float32)

    dma = pltpu.SemaphoreType.DMA
    advanced = pl.pallas_call(
        functools.partial(kernel, nx, ny),
        out_shape=jax.ShapeDtypeStruct((6,) + cell, jnp.float32),
        in_specs=[in_hbm] * 5,
        out_specs=in_hbm,
        scratch_shapes=[
            f32(3, *cell), f32(3, *cell), vmem(cell, jnp.int32),
            smem(permittivity.shape, jnp.float32), smem(conductivity.shape, jnp.float32),
            f32(2, cy, cz), f32(2, cx, cz),
            f32(3, cy, cz), f32(nx, 3, cy, cz), f32(2, 2, cy, cz), f32(2, nx, 2, cy, cz),
            f32(ns, 3 * rows, cz), f32(ny, 3 * rows, cz),
            f32(2, ns, 2 * rows, cz), f32(2, ny, 2 * rows, cz),
            f32(2, ny, 2 * rows, cz), f32(2, ns, 2 * rows, cz), f32(3, ny + 1, rows, cz),
            f32(nx + 1, cy, cz), f32(nx + 1, cy, cz), f32(*cell), f32(3, cx, cz),
            f32(cz // 128, cx * cy, 128), f32(cz, cx * cy), f32(6, *cell),
            dma((5,)), dma((6,)), dma((4,)), dma((4,)), dma((3,)), dma((3,)), dma((5,)), dma((5,)),
        ],
        compiler_params=pltpu.CompilerParams(
            collective_id=0, has_side_effects=True, vmem_limit_bytes=62 * 1024 * 1024
        ),
    )(electric, magnetic, material, permittivity, conductivity)
    return advanced[:3], advanced[3:]


def solution(mesh):
    nx, ny = mesh.shape["gx"], mesh.shape["gy"]
    return jax.shard_map(
        functools.partial(per_device, nx, ny),
        mesh=mesh,
        in_specs=(
            P(None, "gx", "gy", None),
            P(None, "gx", "gy", None),
            P("gx", "gy", None),
            P(),
            P(),
        ),
        out_specs=(P(None, "gx", "gy", None), P(None, "gx", "gy", None)),
        check_vma=False,
    )
```
